32 devices in a mesh: groups: 2 (over y), seq: 4 (over z), head: 4 (over x, core).
Axes of the slice: x: 2, y: 2, z: 4, core: 2. Of those that a mesh axis runs over, the one named last changes fastest.
Arguments:
- segment_query: bfloat16 [512, 4096], P(('groups', 'seq'), 'head'), parts along dimension 0, may hold values from -8 to 8
- segment_memory: bfloat16 [512, 2, 1024], P(('groups', 'seq'), None, 'head'), parts along dimension 0, may hold values from -8 to 8
- finished_memory: bfloat16 [2048, 2, 1024], P(('groups', 'seq'), None, 'head'), parts along dimension 0, may hold values from -8 to 8
- cache_memory: bfloat16 [32768, 2, 1024], P(('groups', 'seq'), None, 'head'), parts along dimension 0, may hold values from -8 to 8
- block_mask: int32 [4, 128], P('groups', 'seq'), parts along dimension 0, may hold values 0 or 1
- owner_index: int32 [2], P('groups'), parts along dimension 0, may hold values from 0 to 3
- valid_count: int32 [2], P('groups'), parts along dimension 0, may hold values from 1 to 256
- output_weight: bfloat16 [4096, 4096], P('head', 'seq'), may hold values from -0.09375 to 0.09375
Outputs:
- mixed_output: float32 [512, 4096], P(('groups', 'head'), 'seq'), parts along dimension 0
The draws below stay inside these ranges and needn't reach their ends.
There are 2 independent parts, one for each index of `groups`. The reference program is written for one: setup_inputs(seed, part) draws one part's arguments, and reference() takes and returns one part's arrays. A program takes and returns all parts, laid end to end along the dimension named above; an argument that names none is the same for every part. Nothing has to cross between parts.
All inputs are finite; a program needn't handle non-finite values. No bound on the sum of `block_mask` on one device may be relied on, other than what follows from the above.
Results may differ from the reference program's by a relative error of at most 0.0065.
Values may be sent and summed in bfloat16 or wider, within the bound.
A program may use at most 128 MiB of HBM per device.

```python
import jax
import jax.numpy as jnp
from jax import lax

D = 4096
HEADS = 32
KV_HEADS = 8
HD = 128
BLOCK = 128
SEGMENT = 256
CONTEXT = 16384
SLOTS = 1024
QBLOCKS = 2
KBLOCKS = 128
N_SEQ = 4


def draw_segment_query(key, part):
    fresh_key = jax.random.fold_in(key, 11)
    values = jnp.clip(1.75 * jax.random.normal(fresh_key, (SEGMENT, HEADS * HD), jnp.float32), -8.0, 8.0)
    return values.astype(jnp.bfloat16)


def draw_segment_memory(key, part):
    fresh_key = jax.random.fold_in(key, 13)
    values = jnp.clip(1.75 * jax.random.normal(fresh_key, (SEGMENT, 2, KV_HEADS * HD), jnp.float32), -8.0, 8.0)
    return values.astype(jnp.bfloat16)


def set_ends(drawn, rng, smallest, largest):
    extent = drawn.shape
    spot = [jax.random.randint(jax.random.fold_in(rng, axis), (), 0, extent[axis]) for axis in range(len(extent))]
    drawn = drawn.at[tuple(spot)].set(smallest)
    longest = extent.index(max(extent))
    spot[longest] = (spot[longest] + 1) % extent[longest]
    return drawn.at[tuple(spot)].set(largest)


def block_levels(stream_key, extent, cuts, smallest, largest):
    level = 1.0
    for dim, parts in cuts:
        draws = jax.random.uniform(jax.random.fold_in(jax.random.fold_in(stream_key, 6), dim), (parts,), jnp.float32, smallest / len(cuts), largest / len(cuts))
        level = level * jnp.repeat(jnp.exp(draws), extent[dim] // parts).reshape((-1,) + (1,) * (len(extent) - 1 - dim))
    return level


def scatter_about(key, shape, width, reach, pieces=(), dtype=jnp.bfloat16):
    values = jax.random.normal(key, shape, jnp.float32) * width
    if len(pieces) > 0:
        values = block_levels(key, shape, pieces, -0.22, 0.18) * values
    return jnp.clip(values, min=-reach, max=reach).astype(dtype)


def setup_inputs(seed: int = 0, part: int = 0) -> dict:
    arg_keys = jax.random.split(jax.random.key(seed), 9)
    own_keys = jax.random.split(jax.random.fold_in(arg_keys[8], part), 9)
    return {
        "segment_query": draw_segment_query(jax.random.fold_in(jax.random.fold_in(arg_keys[8], part), 71), part),
        "segment_memory": draw_segment_memory(jax.random.fold_in(jax.random.fold_in(arg_keys[8], part), 71), part),
        "finished_memory": scatter_about(own_keys[2], (SLOTS, 2, KV_HEADS * HD), 1.75, 8.0, ((0, 4), (2, 4))),
        "cache_memory": scatter_about(own_keys[3], (CONTEXT, 2, KV_HEADS * HD), 1.75, 8.0, ((0, 4), (2, 4))),
        "block_mask": set_ends((jax.random.randint(own_keys[4], (QBLOCKS, KBLOCKS), 0, 3) < 1).astype(jnp.int32), jax.random.fold_in(own_keys[4], 1), 0, 1),
        "owner_index": jax.random.randint(own_keys[5], (1,), 0, N_SEQ).astype(jnp.int32),
        "valid_count": jax.random.randint(own_keys[6], (1,), 1, SEGMENT + 1).astype(jnp.int32),
        "output_weight": scatter_about(arg_keys[7], (HEADS * HD, D), (HEADS * HD) ** -0.5, 0.09375, ((0, 4), (1, 4))),
    }


def reference(segment_query, segment_memory, finished_memory, cache_memory, block_mask, owner_index, valid_count, output_weight):
    group_size = HEADS // KV_HEADS
    slot_start = (owner_index[0] * SEGMENT).astype(jnp.int32)
    finished = lax.dynamic_slice_in_dim(finished_memory, slot_start, SEGMENT, 0)
    pairs = jnp.concatenate([cache_memory, finished, segment_memory], axis=0)
    key_rows = pairs[:, 0].reshape(-1, KV_HEADS, HD)
    value_rows = pairs[:, 1].reshape(-1, KV_HEADS, HD)
    context_ok = jnp.repeat(jnp.repeat(block_mask > 0, BLOCK, axis=0), BLOCK, axis=1)
    positions = jnp.arange(2 * SEGMENT)
    recent_ok = positions < SEGMENT + valid_count[0]
    allowed = jnp.concatenate([context_ok, jnp.broadcast_to(recent_ok[None, :], (SEGMENT, 2 * SEGMENT))], axis=1)
    queries = segment_query.reshape(SEGMENT, HEADS, HD)

    def one_head(head_number):
        query_rows = lax.dynamic_index_in_dim(queries, head_number, 1, keepdims=False)
        kv_number = head_number // group_size
        keys_here = lax.dynamic_index_in_dim(key_rows, kv_number, 1, keepdims=False)
        values_here = lax.dynamic_index_in_dim(value_rows, kv_number, 1, keepdims=False)
        scores = jnp.dot(query_rows, keys_here.T, preferred_element_type=jnp.float32) * (HD ** -0.5)
        scores = jnp.where(allowed, scores, -1.0e30)
        row_peak = jnp.max(scores, axis=1)
        weights = jnp.where(allowed, jnp.exp(scores - row_peak[:, None]), 0.0)
        row_total = jnp.sum(weights, axis=1)
        summed = jnp.dot(weights.astype(jnp.bfloat16), values_here, preferred_element_type=jnp.float32)
        return (summed / row_total[:, None]).astype(jnp.bfloat16)

    per_head = lax.map(one_head, jnp.arange(HEADS))
    attended = per_head.transpose(1, 0, 2).reshape(SEGMENT, HEADS * HD)
    return jnp.dot(attended, output_weight, preferred_element_type=jnp.float32)
```

```python
import functools

import jax
import jax.numpy as jnp
from jax import lax
from jax.experimental import pallas as pl
from jax.experimental.pallas import tpu as pltpu
from jax.sharding import PartitionSpec as P

HD = 128
BLOCK = 128
TILE = 8
FLOOR = -1e30
CEIL = -1e29
LOG2E = 1.4426950408889634


def split_matrix(tokens):
    row = lax.broadcasted_iota(jnp.int32, (2 * BLOCK, 2 * tokens), 0)
    col = lax.broadcasted_iota(jnp.int32, (2 * BLOCK, 2 * tokens), 1)
    want = jnp.where(row < BLOCK, 2 * row, 2 * (row - BLOCK) + 1)
    return jnp.where(row % BLOCK < tokens, jnp.where(col == want, 1.0, 0.0), 0.0).astype(jnp.bfloat16)


def stack_rows(pieces, rows):
    if rows % 16 == 0:
        return jnp.concatenate(pieces, axis=0)
    wide = [piece.astype(jnp.float32) for piece in pieces]
    return jnp.concatenate(wide, axis=0).astype(jnp.bfloat16)


def kernel(
    n,
    heads,
    q_ref,
    seg_hbm,
    fin_hbm,
    cache_hbm,
    mask_ref,
    owner_ref,
    valid_ref,
    w_hbm,
    out_ref,
    cache_raw,
    fin_raw,
    seg_raw,
    w_buf,
    k_buf,
    v_buf,
    score_buf,
    q_buf,
    part_send,
    part_recv,
    att_buf,
    proj_send,
    proj_recv,
    local_sem,
    q_send_sem,
    q_recv_sem,
    part_send_sem,
    part_recv_sem,
    att_send_sem,
    att_recv_sem,
    proj_send_sem,
    proj_recv_sem,
):
    me = lax.axis_index("seq")
    my_head = lax.axis_index("head")
    rows, width = q_ref.shape
    kv_heads = k_buf.shape[1] // HD
    group = width // (kv_heads * HD)
    context = cache_raw.shape[0]
    finished = fin_raw.shape[0]
    pieces = 4
    piece = context // pieces

    local = [
        pltpu.make_async_copy(
            cache_hbm.at[pl.ds(i * piece, piece)],
            cache_raw.at[pl.ds(i * piece, piece)],
            local_sem.at[i],
        )
        for i in range(pieces)
    ]
    local.append(pltpu.make_async_copy(fin_hbm, fin_raw, local_sem.at[pieces]))
    local.append(pltpu.make_async_copy(seg_hbm, seg_raw, local_sem.at[pieces + 1]))
    local.append(pltpu.make_async_copy(w_hbm, w_buf, local_sem.at[pieces + 2]))
    for copy in local:
        copy.start()

    barrier = pltpu.get_barrier_semaphore()
    for i in range(1, n):
        pl.semaphore_signal(barrier, inc=1, device_id={"seq": lax.rem(me + i, n)})
    for i in range(1, heads):
        pl.semaphore_signal(barrier, inc=1, device_id={"head": lax.rem(my_head + i, heads)})
    pl.semaphore_wait(barrier, n + heads - 2)

    def q_copy(target, owner):
        return pltpu.make_async_remote_copy(
            src_ref=q_ref,
            dst_ref=q_buf.at[owner],
            send_sem=q_send_sem.at[target],
            recv_sem=q_recv_sem.at[owner],
            device_id={"seq": target},
        )

    def part_copy(target, owner):
        return pltpu.make_async_remote_copy(
            src_ref=part_send.at[target],
            dst_ref=part_recv.at[owner],
            send_sem=part_send_sem.at[target],
            recv_sem=part_recv_sem.at[owner],
            device_id={"seq": target},
        )

    def att_copy(target, owner):
        return pltpu.make_async_remote_copy(
            src_ref=att_buf.at[owner],
            dst_ref=att_buf.at[owner],
            send_sem=att_send_sem.at[target],
            recv_sem=att_recv_sem.at[owner],
            device_id={"seq": target},
        )

    def proj_copy(target, owner):
        return pltpu.make_async_remote_copy(
            src_ref=proj_send.at[target],
            dst_ref=proj_recv.at[owner],
            send_sem=proj_send_sem.at[target],
            recv_sem=proj_recv_sem.at[owner],
            device_id={"head": target},
        )

    for i in range(1, n):
        q_copy(lax.rem(me - i + n, n), me).start()
    q_buf[me] = q_ref[...]

    def part_block(matrix, raw, start):
        pair = raw.reshape(2 * raw.shape[0], raw.shape[2])
        split = jnp.dot(matrix, pair, preferred_element_type=jnp.float32).astype(jnp.bfloat16)
        k_buf[pl.ds(start, BLOCK), :] = split[:BLOCK]
        ones = jnp.ones((BLOCK, HD), jnp.bfloat16)
        for kv in range(kv_heads):
            v_buf[kv, pl.ds(start, BLOCK), pl.ds(0, HD)] = split[BLOCK:, kv * HD : (kv + 1) * HD]
            v_buf[kv, pl.ds(start, BLOCK), pl.ds(HD, HD)] = ones

    full = split_matrix(BLOCK)
    for i in range(pieces):
        local[i].wait()

        def part_cache(step, carry, i=i):
            start = pl.multiple_of(i * piece + step * BLOCK, BLOCK)
            part_block(full, cache_raw[pl.ds(start, BLOCK)], start)
            return carry

        lax.fori_loop(0, piece // BLOCK, part_cache, 0, unroll=4)
    local[pieces].wait()
    for i in range(finished // BLOCK):
        part_block(full, fin_raw[pl.ds(i * BLOCK, BLOCK)], context + i * BLOCK)
    local[pieces + 1].wait()
    part_block(split_matrix(rows), seg_raw[...], context + finished)

    lane = lax.broadcasted_iota(jnp.int32, (1, HD), 1)
    finished_bias = jnp.where(owner_ref[0] == me, 0.0, FLOOR)
    fresh_bias = jnp.where(lane < jnp.minimum(valid_ref[0] - me * rows, rows), 0.0, FLOOR)
    cache_blocks = context // BLOCK
    blocks = cache_blocks + finished // BLOCK + 1
    tiles = [range(i, min(i + TILE, blocks)) for i in range(0, blocks, TILE)]
    scale = LOG2E * HD**-0.5
    lanes = lax.broadcasted_iota(jnp.int32, (rows, HD), 1)

    def attend(step, carry):
        chunk = lax.rem(me + step, n)

        @pl.when(step > 0)
        def _():
            q_copy(chunk, chunk).wait_recv()

        query_block = (chunk * rows) // BLOCK
        biases = [jnp.where(mask_ref[query_block, j] > 0, 0.0, FLOOR) for j in range(cache_blocks)]
        biases += [finished_bias] * (finished // BLOCK) + [fresh_bias]
        queries = [
            stack_rows(
                [q_buf[chunk, :, pl.ds((kv * group + g) * HD, HD)] for g in range(group)], rows
            )
            for kv in range(kv_heads)
        ]
        peaks = [None] * kv_heads
        sums = [None] * kv_heads

        def score_tile(kv, tile):
            start, size = tile[0] * BLOCK, len(tile) * BLOCK
            scores = lax.dot_general(
                queries[kv],
                k_buf[pl.ds(start, size), pl.ds(kv * HD, HD)],
                (((1,), (1,)), ((), ())),
                preferred_element_type=jnp.float32,
            )
            for offset, j in enumerate(tile):
                biased = scores[:, offset * BLOCK : (offset + 1) * BLOCK] * scale + biases[j]
                score_buf[kv, :, pl.ds(j * BLOCK, BLOCK)] = biased
                peaks[kv] = biased if peaks[kv] is None else jnp.maximum(peaks[kv], biased)

        def value_tile(kv, peak, tile):
            start, size = tile[0] * BLOCK, len(tile) * BLOCK
            weights = [
                jnp.exp2(score_buf[kv, :, pl.ds(j * BLOCK, BLOCK)] - peak).astype(jnp.bfloat16)
                for j in tile
            ]
            term = jnp.dot(
                jnp.concatenate(weights, axis=1),
                v_buf[kv, pl.ds(start, size), :],
                preferred_element_type=jnp.float32,
            )
            sums[kv] = term if sums[kv] is None else sums[kv] + term

        logs = jnp.zeros((rows, HD), jnp.float32)
        for tile in tiles:
            score_tile(0, tile)
        for kv in range(kv_heads):
            peak = jnp.maximum(jnp.max(peaks[kv], axis=1, keepdims=True), CEIL)
            for tile in tiles:
                value_tile(kv, peak, tile)
                if kv + 1 < kv_heads:
                    score_tile(kv + 1, tile)
            total = sums[kv][:, HD:]
            some = total > 0.0
            safe = jnp.where(some, total, 1.0)
            log_total = jnp.where(some, peak + jnp.log2(safe), FLOOR)
            mean = (sums[kv][:, :HD] / safe).astype(jnp.bfloat16)
            for g in range(group):
                number = kv * group + g
                part_send[chunk, :, pl.ds(number * HD, HD)] = mean[g * rows : (g + 1) * rows]
                logs = jnp.where(lanes % 32 == number, log_total[g * rows : (g + 1) * rows], logs)
        high = logs.astype(jnp.bfloat16).astype(jnp.float32)
        middle = (logs - high).astype(jnp.bfloat16).astype(jnp.float32)
        low = logs - high - middle
        packed = jnp.where(lanes < 32, high, jnp.where(lanes < 64, middle, low))
        part_send[chunk, :, pl.ds(width, HD)] = packed.astype(jnp.bfloat16)

        @pl.when(step > 0)
        def _():
            part_copy(chunk, me).start()

        return carry

    lax.fori_loop(0, n, attend, 0)

    def unpack(ref):
        packed = ref[:, pl.ds(width, HD)].astype(jnp.float32)
        return packed[:, :32] + packed[:, 32:64] + packed[:, 64:96]

    sources = [part_send.at[me]]
    for i in range(1, n):
        peer = lax.rem(me + n - i, n)
        part_copy(peer, peer).wait_recv()
        sources.append(part_recv.at[peer])
    logs = [unpack(source) for source in sources]
    top = functools.reduce(jnp.maximum, logs)
    factors = [jnp.exp2(value - top) for value in logs]
    inverse = 1.0 / functools.reduce(jnp.add, factors)
    factors = [factor * inverse for factor in factors]
    for number in range(width // HD):
        columns = pl.ds(number * HD, HD)
        terms = [
            source[:, columns].astype(jnp.float32) * factor[:, number : number + 1]
            for source, factor in zip(sources, factors)
        ]
        att_buf[me, :, columns] = functools.reduce(jnp.add, terms).astype(jnp.bfloat16)

    for i in range(1, n):
        att_copy(lax.rem(me - i + n, n), me).start()
    local[pieces + 2].wait()

    share = n // heads
    for i in range(heads):
        target = lax.rem(me // share + i, heads)
        for j in range(share):
            peer = target * share + j

            @pl.when(peer != me)
            def _():
                att_copy(peer, peer).wait_recv()

        attended = stack_rows([att_buf[target * share + j] for j in range(share)], rows)
        product = jnp.dot(attended, w_buf[...], preferred_element_type=jnp.float32)

        @pl.when(target == my_head)
        def _():
            out_ref[...] = product

        @pl.when(target != my_head)
        def _():
            proj_send[target] = product.astype(jnp.bfloat16)
            proj_copy(target, my_head).start()

    for i in range(1, heads):
        peer = lax.rem(my_head + i, heads)
        proj_copy(peer, peer).wait_recv()
        out_ref[...] += proj_recv[peer].astype(jnp.float32)

    for i in range(1, n):
        peer = lax.rem(me + i, n)
        q_copy(peer, me).wait_send()
        part_copy(peer, me).wait_send()
        att_copy(peer, me).wait_send()
    for i in range(1, heads):
        proj_copy(lax.rem(my_head + i, heads), my_head).wait_send()


def per_device(n, heads, *args):
    query, segment, finished, cache, mask, owner, valid, weight = args
    rows, width = query.shape
    kv_width = segment.shape[2]
    kv_heads = kv_width // HD
    total = cache.shape[0] + finished.shape[0] + BLOCK
    out_rows = rows * n // heads
    bf16, f32 = jnp.bfloat16, jnp.float32
    hbm = pl.BlockSpec(memory_space=pl.ANY)
    vmem = pl.BlockSpec(memory_space=pltpu.VMEM)
    smem = pl.BlockSpec(memory_space=pltpu.SMEM)
    dma = pltpu.SemaphoreType.DMA
    return pl.pallas_call(
        functools.partial(kernel, n, heads),
        out_shape=jax.ShapeDtypeStruct((out_rows, weight.shape[1]), f32),
        in_specs=[vmem, hbm, hbm, hbm, smem, smem, smem, hbm],
        out_specs=vmem,
        scratch_shapes=[
            pltpu.VMEM(cache.shape, bf16),
            pltpu.VMEM(finished.shape, bf16),
            pltpu.VMEM(segment.shape, bf16),
            pltpu.VMEM(weight.shape, bf16),
            pltpu.VMEM((total, kv_width), bf16),
            pltpu.VMEM((kv_heads, total, 2 * HD), bf16),
            pltpu.VMEM((kv_heads, rows * width // kv_width, total), f32),
            pltpu.VMEM((n, rows, width), bf16),
            pltpu.VMEM((n, rows, width + HD), bf16),
            pltpu.VMEM((n, rows, width + HD), bf16),
            pltpu.VMEM((n, rows, width), bf16),
            pltpu.VMEM((heads, out_rows, weight.shape[1]), bf16),
            pltpu.VMEM((heads, out_rows, weight.shape[1]), bf16),
            dma((7,)),
            dma((n,)),
            dma((n,)),
            dma((n,)),
            dma((n,)),
            dma((n,)),
            dma((n,)),
            dma((heads,)),
            dma((heads,)),
        ],
        compiler_params=pltpu.CompilerParams(
            collective_id=0, has_side_effects=True, vmem_limit_bytes=56 << 20
        ),
    )(query, segment, finished, cache, mask, owner, valid, weight)


def solution(mesh):
    return jax.shard_map(
        functools.partial(per_device, mesh.shape["seq"], mesh.shape["head"]),
        mesh=mesh,
        in_specs=(
            P(("groups", "seq"), "head"),
            P(("groups", "seq"), None, "head"),
            P(("groups", "seq"), None, "head"),
            P(("groups", "seq"), None, "head"),
            P("groups", "seq"),
            P("groups"),
            P("groups"),
            P("head", "seq"),
        ),
        out_specs=P(("groups", "head"), "seq"),
        check_vma=False,
    )
```

```python
import functools

import jax
import jax.numpy as jnp
from jax import lax
from jax.experimental import pallas as pl
from jax.experimental.pallas import tpu as pltpu
from jax.sharding import PartitionSpec as P

HD = 128
BLOCK = 128
TILE = 8
FLOOR = -1e30
CEIL = -1e29
LOG2E = 1.4426950408889634


def split_matrix(tokens):
    row = lax.broadcasted_iota(jnp.int32, (2 * BLOCK, 2 * tokens), 0)
    col = lax.broadcasted_iota(jnp.int32, (2 * BLOCK, 2 * tokens), 1)
    want = jnp.where(row < BLOCK, 2 * row, 2 * (row - BLOCK) + 1)
    return jnp.where(row % BLOCK < tokens, jnp.where(col == want, 1.0, 0.0), 0.0).astype(jnp.bfloat16)


def stack_rows(pieces, rows):
    if rows % 16 == 0:
        return jnp.concatenate(pieces, axis=0)
    wide = [piece.astype(jnp.float32) for piece in pieces]
    return jnp.concatenate(wide, axis=0).astype(jnp.bfloat16)


def kernel(
    n,
    heads,
    q_ref,
    seg_hbm,
    fin_hbm,
    cache_hbm,
    mask_ref,
    owner_ref,
    valid_ref,
    w_hbm,
    out_ref,
    cache_raw,
    fin_raw,
    seg_raw,
    w_buf,
    k_buf,
    v_buf,
    score_buf,
    q_buf,
    part_send,
    part_recv,
    att_buf,
    proj_send,
    proj_recv,
    local_sem,
    q_send_sem,
    q_recv_sem,
    part_send_sem,
    part_recv_sem,
    att_send_sem,
    att_recv_sem,
    proj_send_sem,
    proj_recv_sem,
):
    me = lax.axis_index("seq")
    my_head = lax.axis_index("head")
    rows, width = q_ref.shape
    kv_heads = k_buf.shape[1] // HD
    group = width // (kv_heads * HD)
    context = cache_raw.shape[0]
    finished = fin_raw.shape[0]
    order = [0, *range(n // 2, n), *range(n // 2 - 1, 0, -1)]
    pieces = 4
    piece = context // pieces

    local = [
        pltpu.make_async_copy(
            cache_hbm.at[pl.ds(i * piece, piece)],
            cache_raw.at[pl.ds(i * piece, piece)],
            local_sem.at[i],
        )
        for i in range(pieces)
    ]
    local.append(pltpu.make_async_copy(fin_hbm, fin_raw, local_sem.at[pieces]))
    local.append(pltpu.make_async_copy(seg_hbm, seg_raw, local_sem.at[pieces + 1]))
    local.append(pltpu.make_async_copy(w_hbm, w_buf, local_sem.at[pieces + 2]))
    for copy in local:
        copy.start()

    barrier = pltpu.get_barrier_semaphore()
    for i in range(1, n):
        pl.semaphore_signal(barrier, inc=1, device_id={"seq": lax.rem(me + i, n)})
    for i in range(1, heads):
        pl.semaphore_signal(barrier, inc=1, device_id={"head": lax.rem(my_head + i, heads)})
    pl.semaphore_wait(barrier, n + heads - 2)

    def q_copy(target, owner):
        return pltpu.make_async_remote_copy(
            src_ref=q_ref,
            dst_ref=q_buf.at[owner],
            send_sem=q_send_sem.at[target],
            recv_sem=q_recv_sem.at[owner],
            device_id={"seq": target},
        )

    def part_copy(target, owner):
        return pltpu.make_async_remote_copy(
            src_ref=part_send.at[target],
            dst_ref=part_recv.at[owner],
            send_sem=part_send_sem.at[target],
            recv_sem=part_recv_sem.at[owner],
            device_id={"seq": target},
        )

    def att_copy(target, owner):
        return pltpu.make_async_remote_copy(
            src_ref=att_buf.at[owner],
            dst_ref=att_buf.at[owner],
            send_sem=att_send_sem.at[target ^ owner],
            recv_sem=att_recv_sem.at[owner],
            device_id={"seq": target},
        )

    def proj_copy(target, owner):
        return pltpu.make_async_remote_copy(
            src_ref=proj_send.at[target],
            dst_ref=proj_recv.at[owner],
            send_sem=proj_send_sem.at[target],
            recv_sem=proj_recv_sem.at[owner],
            device_id={"head": target},
        )

    for i in order[1:]:
        q_copy(me ^ i, me).start()
    q_buf[me] = q_ref[...]

    def part_block(matrix, raw, start):
        pair = raw.reshape(2 * raw.shape[0], raw.shape[2])
        split = jnp.dot(matrix, pair, preferred_element_type=jnp.float32).astype(jnp.bfloat16)
        k_buf[pl.ds(start, BLOCK), :] = split[:BLOCK]
        ones = jnp.ones((BLOCK, HD), jnp.bfloat16)
        for kv in range(kv_heads):
            v_buf[kv, pl.ds(start, BLOCK), pl.ds(0, HD)] = split[BLOCK:, kv * HD : (kv + 1) * HD]
            v_buf[kv, pl.ds(start, BLOCK), pl.ds(HD, HD)] = ones

    full = split_matrix(BLOCK)
    for i in range(pieces):
        local[i].wait()

        def part_cache(step, carry, i=i):
            start = pl.multiple_of(i * piece + step * BLOCK, BLOCK)
            part_block(full, cache_raw[pl.ds(start, BLOCK)], start)
            return carry

        lax.fori_loop(0, piece // BLOCK, part_cache, 0, unroll=4)
    local[pieces].wait()
    for i in range(finished // BLOCK):
        part_block(full, fin_raw[pl.ds(i * BLOCK, BLOCK)], context + i * BLOCK)
    local[pieces + 1].wait()
    part_block(split_matrix(rows), seg_raw[...], context + finished)

    lane = lax.broadcasted_iota(jnp.int32, (1, HD), 1)
    finished_bias = jnp.where(owner_ref[0] == me, 0.0, FLOOR)
    fresh_bias = jnp.where(lane < jnp.minimum(valid_ref[0] - me * rows, rows), 0.0, FLOOR)
    cache_blocks = context // BLOCK
    blocks = cache_blocks + finished // BLOCK + 1
    tiles = [range(i, min(i + TILE, blocks)) for i in range(0, blocks, TILE)]
    scale = LOG2E * HD**-0.5
    lanes = lax.broadcasted_iota(jnp.int32, (rows, HD), 1)

    def attend(step, carry):
        distance = jnp.where(step < n // 2 + 1, step + n // 2 - 1, n - step)
        chunk = me ^ jnp.where(step == 0, 0, distance)

        @pl.when(step > 0)
        def _():
            q_copy(chunk, chunk).wait_recv()

        query_block = (chunk * rows) // BLOCK
        biases = [jnp.where(mask_ref[query_block, j] > 0, 0.0, FLOOR) for j in range(cache_blocks)]
        biases += [finished_bias] * (finished // BLOCK) + [fresh_bias]
        queries = [
            stack_rows(
                [q_buf[chunk, :, pl.ds((kv * group + g) * HD, HD)] for g in range(group)], rows
            )
            for kv in range(kv_heads)
        ]
        peaks = [None] * kv_heads
        sums = [None] * kv_heads

        def score_tile(kv, tile):
            start, size = tile[0] * BLOCK, len(tile) * BLOCK
            scores = lax.dot_general(
                queries[kv],
                k_buf[pl.ds(start, size), pl.ds(kv * HD, HD)],
                (((1,), (1,)), ((), ())),
                preferred_element_type=jnp.float32,
            )
            for offset, j in enumerate(tile):
                biased = scores[:, offset * BLOCK : (offset + 1) * BLOCK] * scale + biases[j]
                score_buf[kv, :, pl.ds(j * BLOCK, BLOCK)] = biased
                peaks[kv] = biased if peaks[kv] is None else jnp.maximum(peaks[kv], biased)

        def value_tile(kv, peak, tile):
            start, size = tile[0] * BLOCK, len(tile) * BLOCK
            weights = [
                jnp.exp2(score_buf[kv, :, pl.ds(j * BLOCK, BLOCK)] - peak).astype(jnp.bfloat16)
                for j in tile
            ]
            term = jnp.dot(
                jnp.concatenate(weights, axis=1),
                v_buf[kv, pl.ds(start, size), :],
                preferred_element_type=jnp.float32,
            )
            sums[kv] = term if sums[kv] is None else sums[kv] + term

        logs = jnp.zeros((rows, HD), jnp.float32)
        for tile in tiles:
            score_tile(0, tile)
        for kv in range(kv_heads):
            peak = jnp.maximum(jnp.max(peaks[kv], axis=1, keepdims=True), CEIL)
            for tile in tiles:
                value_tile(kv, peak, tile)
                if kv + 1 < kv_heads:
                    score_tile(kv + 1, tile)
            total = sums[kv][:, HD:]
            some = total > 0.0
            safe = jnp.where(some, total, 1.0)
            log_total = jnp.where(some, peak + jnp.log2(safe), FLOOR)
            mean = (sums[kv][:, :HD] / safe).astype(jnp.bfloat16)
            for g in range(group):
                number = kv * group + g
                part_send[chunk, :, pl.ds(number * HD, HD)] = mean[g * rows : (g + 1) * rows]
                logs = jnp.where(lanes % 32 == number, log_total[g * rows : (g + 1) * rows], logs)
        high = logs.astype(jnp.bfloat16).astype(jnp.float32)
        middle = (logs - high).astype(jnp.bfloat16).astype(jnp.float32)
        low = logs - high - middle
        packed = jnp.where(lanes < 32, high, jnp.where(lanes < 64, middle, low))
        part_send[chunk, :, pl.ds(width, HD)] = packed.astype(jnp.bfloat16)

        @pl.when(step > 0)
        def _():
            part_copy(chunk, me).start()

        return carry

    lax.fori_loop(0, n, attend, 0)

    def unpack(ref):
        packed = ref[:, pl.ds(width, HD)].astype(jnp.float32)
        return packed[:, :32] + packed[:, 32:64] + packed[:, 64:96]

    sources = [part_send.at[me]]
    for i in order[1:]:
        peer = me ^ i
        part_copy(peer, peer).wait_recv()
        sources.append(part_recv.at[peer])
    logs = [unpack(source) for source in sources]
    top = functools.reduce(jnp.maximum, logs)
    factors = [jnp.exp2(value - top) for value in logs]
    inverse = 1.0 / functools.reduce(jnp.add, factors)
    factors = [factor * inverse for factor in factors]
    for number in range(width // HD):
        columns = pl.ds(number * HD, HD)
        terms = [
            source[:, columns].astype(jnp.float32) * factor[:, number : number + 1]
            for source, factor in zip(sources, factors)
        ]
        att_buf[me, :, columns] = functools.reduce(jnp.add, terms).astype(jnp.bfloat16)

    def spread(distance):
        step = (distance & -distance if distance else n) // 2
        while step:
            att_copy(me ^ step, me ^ distance).start()
            step //= 2

    spread(0)
    local[pieces + 2].wait()

    share = n // heads
    routes = sorted(range(1, n), key=lambda d: (d.bit_count(), -d))
    if share > 1:
        for distance in routes:
            att_copy(me ^ distance, me ^ distance).wait_recv()
            spread(distance)
    for i in [0] + sorted(range(1, heads), key=lambda d: (d.bit_count(), -d)):
        target = (me // share) ^ i
        if share == 1 and i > 0:
            att_copy(me ^ i, me ^ i).wait_recv()
            spread(i)

        attended = stack_rows([att_buf[target * share + j] for j in range(share)], rows)
        product = jnp.dot(attended, w_buf[...], preferred_element_type=jnp.float32)

        @pl.when(target == my_head)
        def _():
            out_ref[...] = product

        @pl.when(target != my_head)
        def _():
            proj_send[target] = product.astype(jnp.bfloat16)
            proj_copy(target, my_head).start()

    for i in range(1, heads):
        peer = lax.rem(my_head + i, heads)
        proj_copy(peer, peer).wait_recv()
        out_ref[...] += proj_recv[peer].astype(jnp.float32)

    for i in range(1, n):
        peer = lax.rem(me + i, n)
        q_copy(peer, me).wait_send()
        part_copy(peer, me).wait_send()
        att_copy(me ^ i, me).wait_send()
    for i in range(1, heads):
        proj_copy(lax.rem(my_head + i, heads), my_head).wait_send()


def per_device(n, heads, *args):
    query, segment, finished, cache, mask, owner, valid, weight = args
    rows, width = query.shape
    kv_width = segment.shape[2]
    kv_heads = kv_width // HD
    total = cache.shape[0] + finished.shape[0] + BLOCK
    out_rows = rows * n // heads
    bf16, f32 = jnp.bfloat16, jnp.float32
    hbm = pl.BlockSpec(memory_space=pl.ANY)
    vmem = pl.BlockSpec(memory_space=pltpu.VMEM)
    smem = pl.BlockSpec(memory_space=pltpu.SMEM)
    dma = pltpu.SemaphoreType.DMA
    return pl.pallas_call(
        functools.partial(kernel, n, heads),
        out_shape=jax.ShapeDtypeStruct((out_rows, weight.shape[1]), f32),
        in_specs=[vmem, hbm, hbm, hbm, smem, smem, smem, hbm],
        out_specs=vmem,
        scratch_shapes=[
            pltpu.VMEM(cache.shape, bf16),
            pltpu.VMEM(finished.shape, bf16),
            pltpu.VMEM(segment.shape, bf16),
            pltpu.VMEM(weight.shape, bf16),
            pltpu.VMEM((total, kv_width), bf16),
            pltpu.VMEM((kv_heads, total, 2 * HD), bf16),
            pltpu.VMEM((kv_heads, rows * width // kv_width, total), f32),
            pltpu.VMEM((n, rows, width), bf16),
            pltpu.VMEM((n, rows, width + HD), bf16),
            pltpu.VMEM((n, rows, width + HD), bf16),
            pltpu.VMEM((n, rows, width), bf16),
            pltpu.VMEM((heads, out_rows, weight.shape[1]), bf16),
            pltpu.VMEM((heads, out_rows, weight.shape[1]), bf16),
            dma((7,)),
            dma((n,)),
            dma((n,)),
            dma((n,)),
            dma((n,)),
            dma((n,)),
            dma((n,)),
            dma((heads,)),
            dma((heads,)),
        ],
        compiler_params=pltpu.CompilerParams(
            collective_id=0, has_side_effects=True, vmem_limit_bytes=56 << 20
        ),
    )(query, segment, finished, cache, mask, owner, valid, weight)


def solution(mesh):
    return jax.shard_map(
        functools.partial(per_device, mesh.shape["seq"], mesh.shape["head"]),
        mesh=mesh,
        in_specs=(
            P(("groups", "seq"), "head"),
            P(("groups", "seq"), None, "head"),
            P(("groups", "seq"), None, "head"),
            P(("groups", "seq"), None, "head"),
            P("groups", "seq"),
            P("groups"),
            P("groups"),
            P("head", "seq"),
        ),
        out_specs=P(("groups", "head"), "seq"),
        check_vma=False,
    )
```

```python
import functools

import jax
import jax.numpy as jnp
from jax import lax
from jax.experimental import pallas as pl
from jax.experimental.pallas import tpu as pltpu
from jax.sharding import PartitionSpec as P

HD = 128
BLOCK = 128
TILE = 4
DEEP = 8
PAD = 16
FLOOR = -1e30
CEIL = -1e29
LOG2E = 1.4426950408889634


def split_matrix(tokens):
    row = lax.broadcasted_iota(jnp.int32, (2 * BLOCK, 2 * tokens), 0)
    col = lax.broadcasted_iota(jnp.int32, (2 * BLOCK, 2 * tokens), 1)
    want = jnp.where(row < BLOCK, 2 * row, 2 * (row - BLOCK) + 1)
    return jnp.where(row % BLOCK < tokens, jnp.where(col == want, 1.0, 0.0), 0.0).astype(jnp.bfloat16)


def stack_rows(pieces, rows):
    if rows % 16 == 0:
        return jnp.concatenate(pieces, axis=0)
    wide = [piece.astype(jnp.float32) for piece in pieces]
    return jnp.concatenate(wide, axis=0).astype(jnp.bfloat16)


def kernel(
    n,
    heads,
    q_ref,
    seg_hbm,
    fin_hbm,
    cache_hbm,
    mask_ref,
    owner_ref,
    valid_ref,
    w_hbm,
    out_ref,
    cache_raw,
    fin_raw,
    seg_raw,
    w_buf,
    k_buf,
    v_buf,
    score_buf,
    q_buf,
    part_send,
    part_recv,
    att_buf,
    proj_send,
    proj_recv,
    local_sem,
    q_send_sem,
    q_recv_sem,
    part_send_sem,
    part_recv_sem,
    att_send_sem,
    att_recv_sem,
    proj_send_sem,
    proj_recv_sem,
):
    me = lax.axis_index("seq")
    my_head = lax.axis_index("head")
    rows, width = q_ref.shape
    kv_heads = k_buf.shape[1] // HD
    group = width // (kv_heads * HD)
    context = cache_raw.shape[0]
    finished = fin_raw.shape[0]
    order = [0, *range(n // 2, n), *range(n // 2 - 1, 0, -1)]
    pieces = 4
    piece = context // pieces

    local = [
        pltpu.make_async_copy(
            cache_hbm.at[pl.ds(i * piece, piece)],
            cache_raw.at[pl.ds(i * piece, piece)],
            local_sem.at[i],
        )
        for i in range(pieces)
    ]
    local.append(pltpu.make_async_copy(fin_hbm, fin_raw, local_sem.at[pieces]))
    local.append(pltpu.make_async_copy(seg_hbm, seg_raw, local_sem.at[pieces + 1]))
    local.append(pltpu.make_async_copy(w_hbm, w_buf, local_sem.at[pieces + 2]))
    for copy in local:
        copy.start()

    barrier = pltpu.get_barrier_semaphore()
    for i in range(1, n):
        pl.semaphore_signal(barrier, inc=1, device_id={"seq": lax.rem(me + i, n)})
    for i in range(1, heads):
        pl.semaphore_signal(barrier, inc=1, device_id={"head": lax.rem(my_head + i, heads)})
    pl.semaphore_wait(barrier, n + heads - 2)

    def q_copy(target, owner):
        return pltpu.make_async_remote_copy(
            src_ref=q_ref,
            dst_ref=q_buf.at[owner],
            send_sem=q_send_sem.at[target],
            recv_sem=q_recv_sem.at[owner],
            device_id={"seq": target},
        )

    def part_copy(target, owner):
        return pltpu.make_async_remote_copy(
            src_ref=part_send.at[target],
            dst_ref=part_recv.at[owner],
            send_sem=part_send_sem.at[target],
            recv_sem=part_recv_sem.at[owner],
            device_id={"seq": target},
        )

    def att_copy(target, owner):
        return pltpu.make_async_remote_copy(
            src_ref=att_buf.at[owner],
            dst_ref=att_buf.at[owner],
            send_sem=att_send_sem.at[target ^ owner],
            recv_sem=att_recv_sem.at[owner],
            device_id={"seq": target},
        )

    def proj_copy(target, owner):
        return pltpu.make_async_remote_copy(
            src_ref=proj_send.at[target],
            dst_ref=proj_recv.at[owner],
            send_sem=proj_send_sem.at[target],
            recv_sem=proj_recv_sem.at[owner],
            device_id={"head": target},
        )

    for i in order[1:]:
        q_copy(me ^ i, me).start()
    q_buf[me] = q_ref[...]

    def part_block(matrix, raw, start):
        pair = raw.reshape(2 * raw.shape[0], raw.shape[2])
        split = jnp.dot(matrix, pair, preferred_element_type=jnp.float32).astype(jnp.bfloat16)
        k_buf[pl.ds(start, BLOCK), :] = split[:BLOCK]
        for kv in range(kv_heads):
            v_buf[kv, pl.ds(0, HD), pl.ds(start, BLOCK)] = split[BLOCK:, kv * HD : (kv + 1) * HD].T
            v_buf[kv, pl.ds(HD, PAD), pl.ds(start, BLOCK)] = jnp.ones((PAD, BLOCK), jnp.bfloat16)

    full = split_matrix(BLOCK)
    for i in range(pieces):
        local[i].wait()

        def part_cache(step, carry, i=i):
            start = pl.multiple_of(i * piece + step * BLOCK, BLOCK)
            part_block(full, cache_raw[pl.ds(start, BLOCK)], start)
            return carry

        lax.fori_loop(0, piece // BLOCK, part_cache, 0, unroll=4)
    local[pieces].wait()
    for i in range(finished // BLOCK):
        part_block(full, fin_raw[pl.ds(i * BLOCK, BLOCK)], context + i * BLOCK)
    local[pieces + 1].wait()
    part_block(split_matrix(rows), seg_raw[...], context + finished)

    batch = group * rows
    token = lax.broadcasted_iota(jnp.int32, (BLOCK, batch), 0)
    finished_bias = jnp.where(owner_ref[0] == me, 0.0, FLOOR)
    fresh_bias = jnp.where(token < jnp.minimum(valid_ref[0] - me * rows, rows), 0.0, FLOOR)
    cache_blocks = context // BLOCK
    blocks = cache_blocks + finished // BLOCK + 1
    tiles = [range(i, min(i + TILE, blocks)) for i in range(0, blocks, TILE)]
    deep_tiles = [range(i, min(i + DEEP, blocks)) for i in range(0, blocks, DEEP)]
    scale = LOG2E * HD**-0.5
    stat_row = lax.broadcasted_iota(jnp.int32, (PAD, batch), 0)

    def attend(step, carry):
        distance = jnp.where(step < n // 2 + 1, step + n // 2 - 1, n - step)
        chunk = me ^ jnp.where(step == 0, 0, distance)

        @pl.when(step > 0)
        def _():
            q_copy(chunk, chunk).wait_recv()

        query_block = (chunk * rows) // BLOCK
        biases = [jnp.where(mask_ref[query_block, j] > 0, 0.0, FLOOR) for j in range(cache_blocks)]
        biases += [finished_bias] * (finished // BLOCK) + [fresh_bias]
        queries = [
            jnp.concatenate(
                [
                    q_buf[chunk, :, pl.ds((kv * group + g) * HD, HD)].astype(jnp.float32)
                    for g in range(group)
                ],
                axis=0,
            ).T.astype(jnp.bfloat16)
            for kv in range(kv_heads)
        ]
        peaks = [None] * kv_heads
        sums = [None] * kv_heads

        def score_tile(kv, tile):
            start, size = tile[0] * BLOCK, len(tile) * BLOCK
            scores = jnp.dot(
                k_buf[pl.ds(start, size), pl.ds(kv * HD, HD)],
                queries[kv],
                preferred_element_type=jnp.float32,
            )
            for offset, j in enumerate(tile):
                biased = scores[offset * BLOCK : (offset + 1) * BLOCK] * scale + biases[j]
                score_buf[kv, pl.ds(j * BLOCK, BLOCK), :] = biased
                best = jnp.max(biased.reshape(BLOCK // 8, 8, batch), axis=0)
                peaks[kv] = best if peaks[kv] is None else jnp.maximum(peaks[kv], best)

        def value_tile(kv, peak, tile):
            start, size = tile[0] * BLOCK, len(tile) * BLOCK
            weights = [
                jnp.exp2(score_buf[kv, pl.ds(j * BLOCK, BLOCK), :] - peak).astype(jnp.bfloat16)
                for j in tile
            ]
            term = jnp.dot(
                v_buf[kv, :, pl.ds(start, size)],
                jnp.concatenate(weights, axis=0),
                preferred_element_type=jnp.float32,
            )
            sums[kv] = term if sums[kv] is None else sums[kv] + term

        stats = jnp.zeros((PAD, batch), jnp.float32)
        for tile in tiles:
            score_tile(0, tile)
        for kv in range(kv_heads):
            peak = jnp.maximum(jnp.max(peaks[kv], axis=0, keepdims=True), CEIL)
            later = list(tiles) if kv + 1 < kv_heads else []
            for tile in deep_tiles:
                value_tile(kv, peak, tile)
                for ahead in later[: DEEP // TILE]:
                    score_tile(kv + 1, ahead)
                later = later[DEEP // TILE :]
            total = sums[kv][HD : HD + 1]
            some = total > 0.0
            safe = jnp.where(some, total, 1.0)
            log_total = jnp.where(some, peak + jnp.log2(safe), FLOOR)
            mean = sums[kv][:HD] * (1.0 / safe)
            part_send[chunk, pl.ds(kv * HD, HD), :] = mean.astype(jnp.bfloat16)
            high = log_total.astype(jnp.bfloat16).astype(jnp.float32)
            middle = (log_total - high).astype(jnp.bfloat16).astype(jnp.float32)
            for i, value in enumerate((high, middle, log_total - high - middle)):
                stats = jnp.where(stat_row == 3 * kv + i, value, stats)
        part_send[chunk, pl.ds(kv_heads * HD, PAD), :] = stats.astype(jnp.bfloat16)

        @pl.when(step > 0)
        def _():
            part_copy(chunk, me).start()

        return carry

    lax.fori_loop(0, n, attend, 0)

    sources = [part_send.at[me]]
    for i in order[1:]:
        peer = me ^ i
        part_copy(peer, peer).wait_recv()
        sources.append(part_recv.at[peer])
    stats = [source[pl.ds(kv_heads * HD, PAD), :].astype(jnp.float32) for source in sources]
    for kv in range(kv_heads):
        logs = [jnp.sum(stat[3 * kv : 3 * kv + 3], axis=0, keepdims=True) for stat in stats]
        top = functools.reduce(jnp.maximum, logs)
        factors = [jnp.exp2(value - top) for value in logs]
        inverse = 1.0 / functools.reduce(jnp.add, factors)
        terms = [
            source[pl.ds(kv * HD, HD), :].astype(jnp.float32) * (factor * inverse)
            for source, factor in zip(sources, factors)
        ]
        merged = functools.reduce(jnp.add, terms).T
        for g in range(group):
            columns = pl.ds((kv * group + g) * HD, HD)
            att_buf[me, :, columns] = merged[g * rows : (g + 1) * rows].astype(jnp.bfloat16)

    def spread(distance):
        step = (distance & -distance if distance else n) // 2
        while step:
            att_copy(me ^ step, me ^ distance).start()
            step //= 2

    spread(0)
    local[pieces + 2].wait()

    share = n // heads
    routes = sorted(range(1, n), key=lambda d: (d.bit_count(), -d))
    if share > 1:
        for distance in routes:
            att_copy(me ^ distance, me ^ distance).wait_recv()
            spread(distance)
    for i in [0] + sorted(range(1, heads), key=lambda d: (d.bit_count(), -d)):
        target = (me // share) ^ i
        if share == 1 and i > 0:
            att_copy(me ^ i, me ^ i).wait_recv()
            spread(i)

        attended = stack_rows([att_buf[target * share + j] for j in range(share)], rows)
        product = jnp.dot(attended, w_buf[...], preferred_element_type=jnp.float32)

        @pl.when(target == my_head)
        def _():
            out_ref[...] = product

        @pl.when(target != my_head)
        def _():
            proj_send[target] = product.astype(jnp.bfloat16)
            proj_copy(target, my_head).start()

    for i in range(1, heads):
        peer = lax.rem(my_head + i, heads)
        proj_copy(peer, peer).wait_recv()
        out_ref[...] += proj_recv[peer].astype(jnp.float32)

    for i in range(1, n):
        peer = lax.rem(me + i, n)
        q_copy(peer, me).wait_send()
        part_copy(peer, me).wait_send()
        att_copy(me ^ i, me).wait_send()
    for i in range(1, heads):
        proj_copy(lax.rem(my_head + i, heads), my_head).wait_send()


def per_device(n, heads, *args):
    query, segment, finished, cache, mask, owner, valid, weight = args
    rows, width = query.shape
    kv_width = segment.shape[2]
    kv_heads = kv_width // HD
    total = cache.shape[0] + finished.shape[0] + BLOCK
    batch = rows * width // kv_width
    out_rows = rows * n // heads
    bf16, f32 = jnp.bfloat16, jnp.float32
    hbm = pl.BlockSpec(memory_space=pl.ANY)
    vmem = pl.BlockSpec(memory_space=pltpu.VMEM)
    smem = pl.BlockSpec(memory_space=pltpu.SMEM)
    dma = pltpu.SemaphoreType.DMA
    return pl.pallas_call(
        functools.partial(kernel, n, heads),
        out_shape=jax.ShapeDtypeStruct((out_rows, weight.shape[1]), f32),
        in_specs=[vmem, hbm, hbm, hbm, smem, smem, smem, hbm],
        out_specs=vmem,
        scratch_shapes=[
            pltpu.VMEM(cache.shape, bf16),
            pltpu.VMEM(finished.shape, bf16),
            pltpu.VMEM(segment.shape, bf16),
            pltpu.VMEM(weight.shape, bf16),
            pltpu.VMEM((total, kv_width), bf16),
            pltpu.VMEM((kv_heads, HD + PAD, total), bf16),
            pltpu.VMEM((kv_heads, total, batch), f32),
            pltpu.VMEM((n, rows, width), bf16),
            pltpu.VMEM((n, kv_width + PAD, batch), bf16),
            pltpu.VMEM((n, kv_width + PAD, batch), bf16),
            pltpu.VMEM((n, rows, width), bf16),
            pltpu.VMEM((heads, out_rows, weight.shape[1]), bf16),
            pltpu.VMEM((heads, out_rows, weight.shape[1]), bf16),
            dma((7,)),
            dma((n,)),
            dma((n,)),
            dma((n,)),
            dma((n,)),
            dma((n,)),
            dma((n,)),
            dma((heads,)),
            dma((heads,)),
        ],
        compiler_params=pltpu.CompilerParams(
            collective_id=0, has_side_effects=True, vmem_limit_bytes=56 << 20
        ),
    )(query, segment, finished, cache, mask, owner, valid, weight)


def solution(mesh):
    return jax.shard_map(
        functools.partial(per_device, mesh.shape["seq"], mesh.shape["head"]),
        mesh=mesh,
        in_specs=(
            P(("groups", "seq"), "head"),
            P(("groups", "seq"), None, "head"),
            P(("groups", "seq"), None, "head"),
            P(("groups", "seq"), None, "head"),
            P("groups", "seq"),
            P("groups"),
            P("groups"),
            P("head", "seq"),
        ),
        out_specs=P(("groups", "head"), "seq"),
        check_vma=False,
    )
```

```python
import functools

import jax
import jax.numpy as jnp
from jax import lax
from jax.experimental import pallas as pl
from jax.experimental.pallas import tpu as pltpu
from jax.sharding import PartitionSpec as P

HD = 128
BLOCK = 128
TILE = 8
PAD = 16
FLOOR = -1e30
CEIL = -1e29
LOG2E = 1.4426950408889634


def split_matrix(tokens):
    row = lax.broadcasted_iota(jnp.int32, (2 * BLOCK, 2 * tokens), 0)
    col = lax.broadcasted_iota(jnp.int32, (2 * BLOCK, 2 * tokens), 1)
    want = jnp.where(row < BLOCK, 2 * row, 2 * (row - BLOCK) + 1)
    return jnp.where(row % BLOCK < tokens, jnp.where(col == want, 1.0, 0.0), 0.0).astype(jnp.bfloat16)


def stack_rows(pieces, rows):
    if rows % 16 == 0:
        return jnp.concatenate(pieces, axis=0)
    wide = [piece.astype(jnp.float32) for piece in pieces]
    return jnp.concatenate(wide, axis=0).astype(jnp.bfloat16)


def kernel(
    n,
    heads,
    q_ref,
    seg_hbm,
    fin_hbm,
    cache_hbm,
    mask_ref,
    owner_ref,
    valid_ref,
    w_hbm,
    out_ref,
    cache_raw,
    fin_raw,
    seg_raw,
    w_buf,
    k_buf,
    v_buf,
    score_buf,
    q_buf,
    part_send,
    part_recv,
    att_buf,
    prod_buf,
    proj_send,
    proj_recv,
    local_sem,
    q_send_sem,
    q_recv_sem,
    part_send_sem,
    part_recv_sem,
    att_send_sem,
    att_recv_sem,
    proj_send_sem,
    proj_recv_sem,
):
    me = lax.axis_index("seq")
    my_head = lax.axis_index("head")
    rows, width = q_ref.shape
    kv_heads = k_buf.shape[1] // HD
    group = width // (kv_heads * HD)
    context = cache_raw.shape[0]
    finished = fin_raw.shape[0]
    order = [0, *range(n // 2, n), *range(1, n // 2)]
    pieces = 4
    piece = context // pieces

    local = [
        pltpu.make_async_copy(
            cache_hbm.at[pl.ds(i * piece, piece)],
            cache_raw.at[pl.ds(i * piece, piece)],
            local_sem.at[i],
        )
        for i in range(pieces)
    ]
    local.append(pltpu.make_async_copy(fin_hbm, fin_raw, local_sem.at[pieces]))
    local.append(pltpu.make_async_copy(seg_hbm, seg_raw, local_sem.at[pieces + 1]))
    local.append(pltpu.make_async_copy(w_hbm, w_buf, local_sem.at[pieces + 2]))
    for copy in local:
        copy.start()

    chunk_width = width // kv_heads
    for kv in range(kv_heads):
        q_buf[kv, me] = q_ref[:, pl.ds(kv * chunk_width, chunk_width)]

    barrier = pltpu.get_barrier_semaphore()
    for i in range(1, n):
        pl.semaphore_signal(barrier, inc=1, device_id={"seq": lax.rem(me + i, n)})
    for i in range(1, heads):
        pl.semaphore_signal(barrier, inc=1, device_id={"head": lax.rem(my_head + i, heads)})
    pl.semaphore_wait(barrier, n + heads - 2)

    def seq_copy(source, target_buf, sems, kv, mark, target, owner):
        return pltpu.make_async_remote_copy(
            src_ref=source,
            dst_ref=target_buf.at[kv, owner],
            send_sem=sems[0].at[kv, mark],
            recv_sem=sems[1].at[kv, owner],
            device_id={"seq": target},
        )

    def q_copy(kv, target, owner, mark):
        sems = (q_send_sem, q_recv_sem)
        return seq_copy(q_buf.at[kv, owner], q_buf, sems, kv, mark, target, owner)

    def part_copy(kv, target, owner, mark):
        sems = (part_send_sem, part_recv_sem)
        return seq_copy(part_send.at[kv, target], part_recv, sems, kv, mark, target, owner)

    def att_copy(kv, target, owner, mark):
        sems = (att_send_sem, att_recv_sem)
        return seq_copy(att_buf.at[kv, owner], att_buf, sems, kv, mark, target, owner)

    def proj_copy(target, owner):
        return pltpu.make_async_remote_copy(
            src_ref=proj_send.at[target],
            dst_ref=proj_recv.at[owner],
            send_sem=proj_send_sem.at[target],
            recv_sem=proj_recv_sem.at[owner],
            device_id={"head": target},
        )

    bits = [n >> (i + 1) for i in range(n.bit_length() - 1)]
    for kv in range(kv_heads):
        for bit in bits:
            q_copy(kv, me ^ bit, me, bit).start()

    def part_block(matrix, raw, start):
        pair = raw.reshape(2 * raw.shape[0], raw.shape[2])
        split = jnp.dot(matrix, pair, preferred_element_type=jnp.float32).astype(jnp.bfloat16)
        k_buf[pl.ds(start, BLOCK), :] = split[:BLOCK]
        for kv in range(kv_heads):
            v_buf[kv, pl.ds(0, HD), pl.ds(start, BLOCK)] = split[BLOCK:, kv * HD : (kv + 1) * HD].T
            v_buf[kv, pl.ds(HD, PAD), pl.ds(start, BLOCK)] = jnp.ones((PAD, BLOCK), jnp.bfloat16)

    full = split_matrix(BLOCK)
    for i in range(pieces):
        local[i].wait()

        def part_cache(step, carry, i=i):
            start = pl.multiple_of(i * piece + step * BLOCK, BLOCK)
            part_block(full, cache_raw[pl.ds(start, BLOCK)], start)
            return carry

        lax.fori_loop(0, piece // BLOCK, part_cache, 0, unroll=4)
    local[pieces].wait()
    for i in range(finished // BLOCK):
        part_block(full, fin_raw[pl.ds(i * BLOCK, BLOCK)], context + i * BLOCK)
    local[pieces + 1].wait()
    part_block(split_matrix(rows), seg_raw[...], context + finished)

    batch = group * rows
    token = lax.broadcasted_iota(jnp.int32, (BLOCK, batch), 0)
    finished_bias = jnp.where(owner_ref[0] == me, 0.0, FLOOR)
    fresh_bias = jnp.where(token < jnp.minimum(valid_ref[0] - me * rows, rows), 0.0, FLOOR)
    cache_blocks = context // BLOCK
    blocks = cache_blocks + finished // BLOCK + 1
    tiles = [range(i, min(i + TILE, blocks)) for i in range(0, blocks, TILE)]
    scale = LOG2E * HD**-0.5
    stat_row = lax.broadcasted_iota(jnp.int32, (PAD, batch), 0)

    def attend(kv, step, carry):
        distance = jnp.where(step < n // 2 + 1, step + n // 2 - 1, step - n // 2)
        distance = jnp.where(step == 0, 0, distance)
        chunk = me ^ distance

        @pl.when(step > 0)
        def _():
            q_copy(kv, chunk, chunk, distance).wait_recv()

        for bit in bits[1:]:

            @pl.when((step > 0) & (distance % (2 * bit) == 0))
            def _():
                q_copy(kv, me ^ bit, chunk, distance + bit).start()

        query_block = (chunk * rows) // BLOCK
        biases = [jnp.where(mask_ref[query_block, j] > 0, 0.0, FLOOR) for j in range(cache_blocks)]
        biases += [finished_bias] * (finished // BLOCK) + [fresh_bias]
        queries = jnp.concatenate(
            [q_buf[kv, chunk, :, pl.ds(g * HD, HD)].astype(jnp.float32) for g in range(group)],
            axis=0,
        ).T.astype(jnp.bfloat16)

        def score_tile(tile):
            start, size = tile[0] * BLOCK, len(tile) * BLOCK
            scores = jnp.dot(
                k_buf[pl.ds(start, size), pl.ds(kv * HD, HD)],
                queries,
                preferred_element_type=jnp.float32,
            )
            peak = jnp.full((8, batch), CEIL, jnp.float32)
            for offset, j in enumerate(tile):
                biased = scores[offset * BLOCK : (offset + 1) * BLOCK] * scale + biases[j]
                score_buf[pl.ds(j * BLOCK, BLOCK), :] = biased
                peak = jnp.maximum(peak, jnp.max(biased.reshape(BLOCK // 8, 8, batch), axis=0))
            return jnp.max(peak, axis=0, keepdims=True)

        def value_tile(peak, tile):
            start, size = tile[0] * BLOCK, len(tile) * BLOCK
            weights = [
                jnp.exp2(score_buf[pl.ds(j * BLOCK, BLOCK), :] - peak).astype(jnp.bfloat16)
                for j in tile
            ]
            return jnp.dot(
                v_buf[kv, :, pl.ds(start, size)],
                jnp.concatenate(weights, axis=0),
                preferred_element_type=jnp.float32,
            )

        next_peak = score_tile(tiles[0])
        peak, summed = next_peak, None
        for number, tile in enumerate(tiles):
            tile_peak = next_peak
            if number + 1 < len(tiles):
                next_peak = score_tile(tiles[number + 1])
            term = value_tile(tile_peak, tile)
            if summed is None:
                summed = term
            else:
                joined = jnp.maximum(peak, tile_peak)
                summed = summed * jnp.exp2(peak - joined) + term * jnp.exp2(tile_peak - joined)
                peak = joined
        total = summed[HD : HD + 1]
        some = total > 0.0
        safe = jnp.where(some, total, 1.0)
        log_total = jnp.where(some, peak + jnp.log2(safe), FLOOR)
        part_send[kv, chunk, pl.ds(0, HD), :] = (summed[:HD] * (1.0 / safe)).astype(jnp.bfloat16)
        high = log_total.astype(jnp.bfloat16).astype(jnp.float32)
        middle = (log_total - high).astype(jnp.bfloat16).astype(jnp.float32)
        stats = jnp.zeros((PAD, batch), jnp.float32)
        for i, value in enumerate((high, middle, log_total - high - middle)):
            stats = jnp.where(stat_row == i, value, stats)
        part_send[kv, chunk, pl.ds(HD, PAD), :] = stats.astype(jnp.bfloat16)

        @pl.when(step > 0)
        def _():
            part_copy(kv, chunk, me, distance).start()

        if kv > 0:

            @pl.when(step == n // 2)
            def _():
                merge(kv - 1)

        return carry

    def spread(kv, distance):
        step = (distance & -distance if distance else n) // 2
        while step:
            att_copy(kv, me ^ step, me ^ distance, distance + step).start()
            step //= 2

    def merge(kv):
        sources = [part_send.at[kv, me]]
        for i in order[1:]:
            peer = me ^ i
            part_copy(kv, peer, peer, i).wait_recv()
            sources.append(part_recv.at[kv, peer])
        logs = [
            jnp.sum(source[pl.ds(HD, PAD), :].astype(jnp.float32)[:3], axis=0, keepdims=True)
            for source in sources
        ]
        top = functools.reduce(jnp.maximum, logs)
        factors = [jnp.exp2(value - top) for value in logs]
        inverse = 1.0 / functools.reduce(jnp.add, factors)
        terms = [
            source[pl.ds(0, HD), :].astype(jnp.float32) * (factor * inverse)
            for source, factor in zip(sources, factors)
        ]
        merged = functools.reduce(jnp.add, terms).T
        for g in range(group):
            columns = pl.ds(g * HD, HD)
            att_buf[kv, me, :, columns] = merged[g * rows : (g + 1) * rows].astype(jnp.bfloat16)
        spread(kv, 0)

    for kv in range(kv_heads):
        lax.fori_loop(0, n, functools.partial(attend, kv), 0)

    share = n // heads
    last = kv_heads - 1
    arrived = set()

    def collect(kv, distance):
        if distance and (kv, distance) not in arrived:
            arrived.add((kv, distance))
            att_copy(kv, me ^ distance, me ^ distance, distance).wait_recv()
            spread(kv, distance)

    def collect_all(kv):
        for distance in sorted(range(1, n), key=lambda d: (d.bit_count(), -d)):
            collect(kv, distance)

    def project(kv, i):
        target = (me // share) ^ i
        if share == 1:
            collect(kv, i)
        else:
            collect_all(kv)
        attended = stack_rows([att_buf[kv, target * share + j] for j in range(share)], rows)
        product = jnp.dot(
            attended,
            w_buf[pl.ds(kv * chunk_width, chunk_width), :],
            preferred_element_type=jnp.float32,
        )
        if kv > 0:
            product = product + prod_buf[i]
        if kv < last:
            prod_buf[i] = product
            return

        @pl.when(target == my_head)
        def _():
            out_ref[...] = product

        @pl.when(target != my_head)
        def _():
            proj_send[target] = product.astype(jnp.bfloat16)
            proj_copy(target, my_head).start()

    local[pieces + 2].wait()

    head_order = [0] + sorted(range(1, heads), key=lambda d: (d.bit_count(), -d))
    for kv in range(last):
        collect(kv, n // 2)
        project(kv, 0)
    merge(last)
    for kv in range(last):
        for i in head_order[1:]:
            project(kv, i)
    for i in head_order:
        project(last, i)

    for i in range(1, heads):
        peer = lax.rem(my_head + i, heads)
        proj_copy(peer, peer).wait_recv()
        out_ref[...] += proj_recv[peer].astype(jnp.float32)

    for kv in range(kv_heads):
        for i in range(1, n):
            q_copy(kv, me ^ i, me, i).wait_send()
            part_copy(kv, me ^ i, me, i).wait_send()
            att_copy(kv, me ^ i, me, i).wait_send()
    for i in range(1, heads):
        proj_copy(lax.rem(my_head + i, heads), my_head).wait_send()


def per_device(n, heads, *args):
    query, segment, finished, cache, mask, owner, valid, weight = args
    rows, width = query.shape
    kv_width = segment.shape[2]
    kv_heads = kv_width // HD
    total = cache.shape[0] + finished.shape[0] + BLOCK
    batch = rows * width // kv_width
    out_rows = rows * n // heads
    bf16, f32 = jnp.bfloat16, jnp.float32
    hbm = pl.BlockSpec(memory_space=pl.ANY)
    vmem = pl.BlockSpec(memory_space=pltpu.VMEM)
    smem = pl.BlockSpec(memory_space=pltpu.SMEM)
    dma = pltpu.SemaphoreType.DMA
    return pl.pallas_call(
        functools.partial(kernel, n, heads),
        out_shape=jax.ShapeDtypeStruct((out_rows, weight.shape[1]), f32),
        in_specs=[vmem, hbm, hbm, hbm, smem, smem, smem, hbm],
        out_specs=vmem,
        scratch_shapes=[
            pltpu.VMEM(cache.shape, bf16),
            pltpu.VMEM(finished.shape, bf16),
            pltpu.VMEM(segment.shape, bf16),
            pltpu.VMEM(weight.shape, bf16),
            pltpu.VMEM((total, kv_width), bf16),
            pltpu.VMEM((kv_heads, HD + PAD, total), bf16),
            pltpu.VMEM((total, batch), f32),
            pltpu.VMEM((kv_heads, n, rows, width // kv_heads), bf16),
            pltpu.VMEM((kv_heads, n, HD + PAD, batch), bf16),
            pltpu.VMEM((kv_heads, n, HD + PAD, batch), bf16),
            pltpu.VMEM((kv_heads, n, rows, width // kv_heads), bf16),
            pltpu.VMEM((heads, out_rows, weight.shape[1]), f32),
            pltpu.VMEM((heads, out_rows, weight.shape[1]), bf16),
            pltpu.VMEM((heads, out_rows, weight.shape[1]), bf16),
            dma((7,)),
            dma((kv_heads, n)),
            dma((kv_heads, n)),
            dma((kv_heads, n)),
            dma((kv_heads, n)),
            dma((kv_heads, n)),
            dma((kv_heads, n)),
            dma((heads,)),
            dma((heads,)),
        ],
        compiler_params=pltpu.CompilerParams(
            collective_id=0, has_side_effects=True, vmem_limit_bytes=56 << 20
        ),
    )(query, segment, finished, cache, mask, owner, valid, weight)


def solution(mesh):
    return jax.shard_map(
        functools.partial(per_device, mesh.shape["seq"], mesh.shape["head"]),
        mesh=mesh,
        in_specs=(
            P(("groups", "seq"), "head"),
            P(("groups", "seq"), None, "head"),
            P(("groups", "seq"), None, "head"),
            P(("groups", "seq"), None, "head"),
            P("groups", "seq"),
            P("groups"),
            P("groups"),
            P("head", "seq"),
        ),
        out_specs=P(("groups", "head"), "seq"),
        check_vma=False,
    )
```

```python
import functools

import jax
import jax.numpy as jnp
from jax import lax
from jax.experimental import pallas as pl
from jax.experimental.pallas import tpu as pltpu
from jax.sharding import PartitionSpec as P

HD = 128
BLOCK = 128
TILE = 8
SUB = 2
PAD = 16
FLOOR = -1e30
CEIL = -1e29
LOG2E = 1.4426950408889634


def split_matrix(tokens):
    row = lax.broadcasted_iota(jnp.int32, (2 * BLOCK, 2 * tokens), 0)
    col = lax.broadcasted_iota(jnp.int32, (2 * BLOCK, 2 * tokens), 1)
    want = jnp.where(row < BLOCK, 2 * row, 2 * (row - BLOCK) + 1)
    return jnp.where(row % BLOCK < tokens, jnp.where(col == want, 1.0, 0.0), 0.0).astype(jnp.bfloat16)


def stack_rows(pieces, rows):
    if rows % 16 == 0:
        return jnp.concatenate(pieces, axis=0)
    wide = [piece.astype(jnp.float32) for piece in pieces]
    return jnp.concatenate(wide, axis=0).astype(jnp.bfloat16)


def kernel(
    n,
    heads,
    q_ref,
    seg_hbm,
    fin_hbm,
    cache_hbm,
    mask_ref,
    owner_ref,
    valid_ref,
    w_hbm,
    out_ref,
    cache_raw,
    fin_raw,
    seg_raw,
    w_buf,
    k_buf,
    v_buf,
    score_buf,
    q_buf,
    part_send,
    part_recv,
    att_buf,
    prod_buf,
    proj_send,
    proj_recv,
    local_sem,
    q_send_sem,
    q_recv_sem,
    part_send_sem,
    part_recv_sem,
    att_send_sem,
    att_recv_sem,
    proj_send_sem,
    proj_recv_sem,
):
    me = lax.axis_index("seq")
    my_head = lax.axis_index("head")
    rows, width = q_ref.shape
    kv_heads = k_buf.shape[0]
    query_blocks = mask_ref.shape[0]
    group = width // (kv_heads * HD)
    context = cache_raw.shape[0]
    finished = fin_raw.shape[0]
    order = [0, *range(n // 2, n), *range(1, n // 2)]
    pieces = 4
    piece = context // pieces

    local = [
        pltpu.make_async_copy(
            cache_hbm.at[pl.ds(i * piece, piece)],
            cache_raw.at[pl.ds(i * piece, piece)],
            local_sem.at[i],
        )
        for i in range(pieces)
    ]
    local.append(pltpu.make_async_copy(fin_hbm, fin_raw, local_sem.at[pieces]))
    local.append(pltpu.make_async_copy(seg_hbm, seg_raw, local_sem.at[pieces + 1]))
    local.append(pltpu.make_async_copy(w_hbm, w_buf, local_sem.at[pieces + 2]))
    for copy in local:
        copy.start()

    chunk_width = width // kv_heads
    for kv in range(kv_heads):
        q_buf[kv, me] = q_ref[:, pl.ds(kv * chunk_width, chunk_width)]

    barrier = pltpu.get_barrier_semaphore()
    for i in range(1, n):
        pl.semaphore_signal(barrier, inc=1, device_id={"seq": lax.rem(me + i, n)})
    for i in range(1, heads):
        pl.semaphore_signal(barrier, inc=1, device_id={"head": lax.rem(my_head + i, heads)})
    pl.semaphore_wait(barrier, n + heads - 2)

    def seq_copy(source, target_buf, sems, kv, mark, target, owner):
        return pltpu.make_async_remote_copy(
            src_ref=source,
            dst_ref=target_buf.at[kv, owner],
            send_sem=sems[0].at[kv, mark],
            recv_sem=sems[1].at[kv, owner],
            device_id={"seq": target},
        )

    def q_copy(kv, target, owner, mark):
        sems = (q_send_sem, q_recv_sem)
        return seq_copy(q_buf.at[kv, owner], q_buf, sems, kv, mark, target, owner)

    def part_copy(kv, target, owner, mark):
        sems = (part_send_sem, part_recv_sem)
        return seq_copy(part_send.at[kv, target], part_recv, sems, kv, mark, target, owner)

    def att_copy(kv, target, owner, mark):
        sems = (att_send_sem, att_recv_sem)
        return seq_copy(att_buf.at[kv, owner], att_buf, sems, kv, mark, target, owner)

    def proj_copy(target, owner):
        return pltpu.make_async_remote_copy(
            src_ref=proj_send.at[target],
            dst_ref=proj_recv.at[owner],
            send_sem=proj_send_sem.at[target],
            recv_sem=proj_recv_sem.at[owner],
            device_id={"head": target},
        )

    bits = [n >> (i + 1) for i in range(n.bit_length() - 1)]
    for kv in range(kv_heads):
        for bit in bits:
            q_copy(kv, me ^ bit, me, bit).start()

    def part_block(matrix, raw, start, biases):
        pair = raw.reshape(2 * raw.shape[0], raw.shape[2])
        split = jnp.dot(matrix, pair, preferred_element_type=jnp.float32).astype(jnp.bfloat16)
        extra = jnp.zeros((BLOCK, HD), jnp.float32)
        for number, bias in enumerate(biases):
            extra = jnp.where(lane == number, bias, extra)
        extra = extra.astype(jnp.bfloat16)
        for kv in range(kv_heads):
            k_buf[kv, pl.ds(start, BLOCK), pl.ds(0, HD)] = split[:BLOCK, kv * HD : (kv + 1) * HD]
            k_buf[kv, pl.ds(start, BLOCK), pl.ds(HD, HD)] = extra
            v_buf[kv, pl.ds(0, HD), pl.ds(start, BLOCK)] = split[BLOCK:, kv * HD : (kv + 1) * HD].T
            v_buf[kv, pl.ds(HD, PAD), pl.ds(start, BLOCK)] = jnp.ones((PAD, BLOCK), jnp.bfloat16)

    lane = lax.broadcasted_iota(jnp.int32, (BLOCK, HD), 1)
    token = lax.broadcasted_iota(jnp.int32, (BLOCK, HD), 0)
    finished_bias = jnp.where(owner_ref[0] == me, 0.0, FLOOR)
    fresh_bias = jnp.where(token < jnp.minimum(valid_ref[0] - me * rows, rows), 0.0, FLOOR)
    full = split_matrix(BLOCK)
    for i in range(pieces):
        local[i].wait()

        def part_cache(step, carry, i=i):
            start = pl.multiple_of(i * piece + step * BLOCK, BLOCK)
            number = i * (piece // BLOCK) + step
            biases = [
                jnp.where(mask_ref[row, number] > 0, 0.0, FLOOR) for row in range(query_blocks)
            ]
            part_block(full, cache_raw[pl.ds(start, BLOCK)], start, biases)
            return carry

        lax.fori_loop(0, piece // BLOCK, part_cache, 0, unroll=4)
    local[pieces].wait()
    for i in range(finished // BLOCK):
        start = context + i * BLOCK
        part_block(full, fin_raw[pl.ds(i * BLOCK, BLOCK)], start, [finished_bias] * query_blocks)
    local[pieces + 1].wait()
    start = context + finished
    part_block(split_matrix(rows), seg_raw[...], start, [fresh_bias] * query_blocks)

    batch = group * rows
    blocks = (context + finished) // BLOCK + 1
    tiles = [range(i, min(i + TILE, blocks)) for i in range(0, blocks, TILE)]
    scale = LOG2E * HD**-0.5
    stat_row = lax.broadcasted_iota(jnp.int32, (PAD, batch), 0)

    def attend(kv, step, carry):
        distance = jnp.where(step < n // 2 + 1, step + n // 2 - 1, step - n // 2)
        distance = jnp.where(step == 0, 0, distance)
        chunk = me ^ distance

        @pl.when(step > 0)
        def _():
            q_copy(kv, chunk, chunk, distance).wait_recv()

        for bit in bits[1:]:

            @pl.when((step > 0) & (distance % (2 * bit) == 0))
            def _():
                q_copy(kv, me ^ bit, chunk, distance + bit).start()

        query_block = (chunk * rows) // BLOCK
        queries = jnp.concatenate(
            [q_buf[kv, chunk, :, pl.ds(g * HD, HD)].astype(jnp.float32) for g in range(group)],
            axis=0,
        ).T
        mark = lax.broadcasted_iota(jnp.int32, (HD, batch), 0) == query_block
        queries = jnp.concatenate([queries, jnp.where(mark, 1.0, 0.0)], axis=0)
        queries = queries.astype(jnp.bfloat16)

        def score_tile(peak, tile):
            start, size = tile[0] * BLOCK, len(tile) * BLOCK
            scores = jnp.dot(
                k_buf[kv, pl.ds(start, size), :], queries, preferred_element_type=jnp.float32
            )
            score_buf[pl.ds(start, size), :] = scores
            return jnp.maximum(peak, jnp.max(scores.reshape(size // 8, 8, batch), axis=0))

        def value_tile(peak, tile):
            start, size = tile[0] * BLOCK, len(tile) * BLOCK
            weights = jnp.exp2((score_buf[pl.ds(start, size), :] - peak) * scale)
            return jnp.dot(
                v_buf[kv, :, pl.ds(start, size)],
                weights.astype(jnp.bfloat16),
                preferred_element_type=jnp.float32,
            )

        def cut(tile):
            return [tile[i : i + SUB] for i in range(0, len(tile), SUB)]

        floor = jnp.full((8, batch), CEIL, jnp.float32)
        ahead = floor
        for part in cut(tiles[0]):
            ahead = score_tile(ahead, part)
        peak, summed = None, None
        for number, tile in enumerate(tiles):
            tile_peak = jnp.max(ahead, axis=0, keepdims=True)
            ahead, later = floor, cut(tiles[number + 1]) if number + 1 < len(tiles) else []
            term = None
            for part in cut(tile):
                if later:
                    ahead = score_tile(ahead, later.pop(0))
                piece_term = value_tile(tile_peak, part)
                term = piece_term if term is None else term + piece_term
            for part in later:
                ahead = score_tile(ahead, part)
            if summed is None:
                peak, summed = tile_peak, term
            else:
                joined = jnp.maximum(peak, tile_peak)
                old, new = jnp.exp2((peak - joined) * scale), jnp.exp2((tile_peak - joined) * scale)
                summed = summed * old + term * new
                peak = joined
        total = summed[HD : HD + 1]
        some = total > 0.0
        safe = jnp.where(some, total, 1.0)
        log_total = jnp.where(some, peak * scale + jnp.log2(safe), FLOOR)
        part_send[kv, chunk, pl.ds(0, HD), :] = (summed[:HD] * (1.0 / safe)).astype(jnp.bfloat16)
        high = log_total.astype(jnp.bfloat16).astype(jnp.float32)
        middle = (log_total - high).astype(jnp.bfloat16).astype(jnp.float32)
        stats = jnp.zeros((PAD, batch), jnp.float32)
        for i, value in enumerate((high, middle, log_total - high - middle)):
            stats = jnp.where(stat_row == i, value, stats)
        part_send[kv, chunk, pl.ds(HD, PAD), :] = stats.astype(jnp.bfloat16)

        @pl.when(step > 0)
        def _():
            part_copy(kv, chunk, me, distance).start()

        if kv > 0:

            @pl.when(step == n // 2)
            def _():
                merge(kv - 1)

        return carry

    def spread(kv, distance):
        step = (distance & -distance if distance else n) // 2
        while step:
            att_copy(kv, me ^ step, me ^ distance, distance + step).start()
            step //= 2

    def merge(kv):
        sources = [part_send.at[kv, me]]
        for i in order[1:]:
            peer = me ^ i
            part_copy(kv, peer, peer, i).wait_recv()
            sources.append(part_recv.at[kv, peer])
        logs = [
            jnp.sum(source[pl.ds(HD, PAD), :].astype(jnp.float32)[:3], axis=0, keepdims=True)
            for source in sources
        ]
        top = functools.reduce(jnp.maximum, logs)
        factors = [jnp.exp2(value - top) for value in logs]
        inverse = 1.0 / functools.reduce(jnp.add, factors)
        terms = [
            source[pl.ds(0, HD), :].astype(jnp.float32) * (factor * inverse)
            for source, factor in zip(sources, factors)
        ]
        merged = functools.reduce(jnp.add, terms).T
        for g in range(group):
            columns = pl.ds(g * HD, HD)
            att_buf[kv, me, :, columns] = merged[g * rows : (g + 1) * rows].astype(jnp.bfloat16)
        spread(kv, 0)

    for kv in range(kv_heads):
        lax.fori_loop(0, n, functools.partial(attend, kv), 0)

    share = n // heads
    last = kv_heads - 1
    arrived = set()

    def collect(kv, distance):
        if distance and (kv, distance) not in arrived:
            arrived.add((kv, distance))
            att_copy(kv, me ^ distance, me ^ distance, distance).wait_recv()
            spread(kv, distance)

    def collect_all(kv):
        for distance in sorted(range(1, n), key=lambda d: (d.bit_count(), -d)):
            collect(kv, distance)

    def project(kv, i):
        target = (me // share) ^ i
        if share == 1:
            collect(kv, i)
        else:
            collect_all(kv)
        attended = stack_rows([att_buf[kv, target * share + j] for j in range(share)], rows)
        product = jnp.dot(
            attended,
            w_buf[pl.ds(kv * chunk_width, chunk_width), :],
            preferred_element_type=jnp.float32,
        )
        if kv > 0:
            product = product + prod_buf[i]
        if kv < last:
            prod_buf[i] = product
            return

        @pl.when(target == my_head)
        def _():
            out_ref[...] = product

        @pl.when(target != my_head)
        def _():
            proj_send[target] = product.astype(jnp.bfloat16)
            proj_copy(target, my_head).start()

    local[pieces + 2].wait()

    head_order = [0] + sorted(range(1, heads), key=lambda d: (d.bit_count(), -d))
    for kv in range(last):
        collect(kv, n // 2)
        project(kv, 0)
    merge(last)
    for kv in range(last):
        for i in head_order[1:]:
            project(kv, i)
    for i in head_order:
        project(last, i)

    for i in range(1, heads):
        peer = lax.rem(my_head + i, heads)
        proj_copy(peer, peer).wait_recv()
        out_ref[...] += proj_recv[peer].astype(jnp.float32)

    for kv in range(kv_heads):
        for i in range(1, n):
            q_copy(kv, me ^ i, me, i).wait_send()
            part_copy(kv, me ^ i, me, i).wait_send()
            att_copy(kv, me ^ i, me, i).wait_send()
    for i in range(1, heads):
        proj_copy(lax.rem(my_head + i, heads), my_head).wait_send()


def per_device(n, heads, *args):
    query, segment, finished, cache, mask, owner, valid, weight = args
    rows, width = query.shape
    kv_width = segment.shape[2]
    kv_heads = kv_width // HD
    total = cache.shape[0] + finished.shape[0] + BLOCK
    batch = rows * width // kv_width
    out_rows = rows * n // heads
    bf16, f32 = jnp.bfloat16, jnp.float32
    hbm = pl.BlockSpec(memory_space=pl.ANY)
    vmem = pl.BlockSpec(memory_space=pltpu.VMEM)
    smem = pl.BlockSpec(memory_space=pltpu.SMEM)
    dma = pltpu.SemaphoreType.DMA
    return pl.pallas_call(
        functools.partial(kernel, n, heads),
        out_shape=jax.ShapeDtypeStruct((out_rows, weight.shape[1]), f32),
        in_specs=[vmem, hbm, hbm, hbm, smem, smem, smem, hbm],
        out_specs=vmem,
        scratch_shapes=[
            pltpu.VMEM(cache.shape, bf16),
            pltpu.VMEM(finished.shape, bf16),
            pltpu.VMEM(segment.shape, bf16),
            pltpu.VMEM(weight.shape, bf16),
            pltpu.VMEM((kv_heads, total, 2 * HD), bf16),
            pltpu.VMEM((kv_heads, HD + PAD, total), bf16),
            pltpu.VMEM((total, batch), f32),
            pltpu.VMEM((kv_heads, n, rows, width // kv_heads), bf16),
            pltpu.VMEM((kv_heads, n, HD + PAD, batch), bf16),
            pltpu.VMEM((kv_heads, n, HD + PAD, batch), bf16),
            pltpu.VMEM((kv_heads, n, rows, width // kv_heads), bf16),
            pltpu.VMEM((heads, out_rows, weight.shape[1]), f32),
            pltpu.VMEM((heads, out_rows, weight.shape[1]), bf16),
            pltpu.VMEM((heads, out_rows, weight.shape[1]), bf16),
            dma((7,)),
            dma((kv_heads, n)),
            dma((kv_heads, n)),
            dma((kv_heads, n)),
            dma((kv_heads, n)),
            dma((kv_heads, n)),
            dma((kv_heads, n)),
            dma((heads,)),
            dma((heads,)),
        ],
        compiler_params=pltpu.CompilerParams(
            collective_id=0, has_side_effects=True, vmem_limit_bytes=56 << 20
        ),
    )(query, segment, finished, cache, mask, owner, valid, weight)


def solution(mesh):
    return jax.shard_map(
        functools.partial(per_device, mesh.shape["seq"], mesh.shape["head"]),
        mesh=mesh,
        in_specs=(
            P(("groups", "seq"), "head"),
            P(("groups", "seq"), None, "head"),
            P(("groups", "seq"), None, "head"),
            P(("groups", "seq"), None, "head"),
            P("groups", "seq"),
            P("groups"),
            P("groups"),
            P("head", "seq"),
        ),
        out_specs=P(("groups", "head"), "seq"),
        check_vma=False,
    )
```

```python
import functools

import jax
import jax.numpy as jnp
from jax import lax
from jax.experimental import pallas as pl
from jax.experimental.pallas import tpu as pltpu
from jax.sharding import PartitionSpec as P

HD = 128
BLOCK = 128
TILE = 8
SUB = 2
PAD = 16
FLOOR = -1e30
CEIL = -1e29
LOG2E = 1.4426950408889634


def split_matrix(tokens):
    row = lax.broadcasted_iota(jnp.int32, (2 * BLOCK, 2 * tokens), 0)
    col = lax.broadcasted_iota(jnp.int32, (2 * BLOCK, 2 * tokens), 1)
    want = jnp.where(row < BLOCK, 2 * row, 2 * (row - BLOCK) + 1)
    return jnp.where(row % BLOCK < tokens, jnp.where(col == want, 1.0, 0.0), 0.0).astype(jnp.bfloat16)


def stack_rows(pieces, rows):
    if rows % 16 == 0:
        return jnp.concatenate(pieces, axis=0)
    wide = [piece.astype(jnp.float32) for piece in pieces]
    return jnp.concatenate(wide, axis=0).astype(jnp.bfloat16)


def kernel(
    n,
    heads,
    q_ref,
    seg_hbm,
    fin_hbm,
    cache_hbm,
    mask_ref,
    owner_ref,
    valid_ref,
    w_hbm,
    out_ref,
    cache_raw,
    fin_raw,
    seg_raw,
    w_buf,
    k_buf,
    v_buf,
    score_buf,
    q_buf,
    part_send,
    part_recv,
    att_buf,
    prod_buf,
    proj_send,
    proj_recv,
    local_sem,
    q_send_sem,
    q_recv_sem,
    part_send_sem,
    part_recv_sem,
    att_send_sem,
    att_recv_sem,
    proj_send_sem,
    proj_recv_sem,
):
    me = lax.axis_index("seq")
    my_head = lax.axis_index("head")
    rows, width = q_ref.shape
    kv_heads = k_buf.shape[0]
    query_blocks = mask_ref.shape[0]
    group = width // (kv_heads * HD)
    context = cache_raw.shape[0]
    finished = fin_raw.shape[0]
    order = [0, *range(n // 2, n), *range(1, n // 2)]
    pieces = 4
    piece = context // pieces

    local = [
        pltpu.make_async_copy(
            cache_hbm.at[pl.ds(i * piece, piece)],
            cache_raw.at[pl.ds(i * piece, piece)],
            local_sem.at[i],
        )
        for i in range(pieces)
    ]
    local.append(pltpu.make_async_copy(fin_hbm, fin_raw, local_sem.at[pieces]))
    local.append(pltpu.make_async_copy(seg_hbm, seg_raw, local_sem.at[pieces + 1]))
    local.append(pltpu.make_async_copy(w_hbm, w_buf, local_sem.at[pieces + 2]))
    for copy in local:
        copy.start()

    chunk_width = width // kv_heads
    for kv in range(kv_heads):
        q_buf[kv, me] = q_ref[:, pl.ds(kv * chunk_width, chunk_width)]

    barrier = pltpu.get_barrier_semaphore()
    for i in range(1, n):
        pl.semaphore_signal(barrier, inc=1, device_id={"seq": lax.rem(me + i, n)})
    for i in range(1, heads):
        pl.semaphore_signal(barrier, inc=1, device_id={"head": lax.rem(my_head + i, heads)})
    pl.semaphore_wait(barrier, n + heads - 2)

    def seq_copy(source, target_buf, sems, kv, mark, target, owner):
        return pltpu.make_async_remote_copy(
            src_ref=source,
            dst_ref=target_buf.at[kv, owner],
            send_sem=sems[0].at[kv, mark],
            recv_sem=sems[1].at[kv, owner],
            device_id={"seq": target},
        )

    def q_copy(kv, target, owner, mark):
        sems = (q_send_sem, q_recv_sem)
        return seq_copy(q_buf.at[kv, owner], q_buf, sems, kv, mark, target, owner)

    half = n // 2

    def keeper(chunk):
        return jnp.where(chunk < half, half - 1, half)

    def part_copy(kv, chunk, source):
        slot = lax.rem(chunk, half)
        return pltpu.make_async_remote_copy(
            src_ref=part_send.at[kv, chunk],
            dst_ref=part_recv.at[kv, slot, source],
            send_sem=part_send_sem.at[kv, chunk],
            recv_sem=part_recv_sem.at[kv, slot, source],
            device_id={"seq": keeper(chunk)},
        )

    def att_copy(kv, chunk, side):
        return pltpu.make_async_remote_copy(
            src_ref=att_buf.at[kv, chunk],
            dst_ref=att_buf.at[kv, chunk],
            send_sem=att_send_sem.at[side, kv, chunk],
            recv_sem=att_recv_sem.at[kv, chunk],
            device_id={"seq": lax.rem(me + (n - 1 if side == 0 else 1), n)},
        )

    def att_sides(chunk):
        middle = keeper(chunk)
        return ((me <= middle) & (me > 0), (me >= middle) & (me < n - 1))

    def spread(kv, chunk):
        for side, goes in enumerate(att_sides(chunk)):

            @pl.when(goes)
            def _():
                att_copy(kv, chunk, side).start()

    def proj_copy(target, owner):
        return pltpu.make_async_remote_copy(
            src_ref=proj_send.at[target],
            dst_ref=proj_recv.at[owner],
            send_sem=proj_send_sem.at[target],
            recv_sem=proj_recv_sem.at[owner],
            device_id={"head": target},
        )

    bits = [n >> (i + 1) for i in range(n.bit_length() - 1)]
    for kv in range(kv_heads):
        for bit in bits:
            q_copy(kv, me ^ bit, me, bit).start()

    def part_block(matrix, raw, start, biases):
        pair = raw.reshape(2 * raw.shape[0], raw.shape[2])
        split = jnp.dot(matrix, pair, preferred_element_type=jnp.float32).astype(jnp.bfloat16)
        extra = jnp.zeros((BLOCK, HD), jnp.float32)
        for number, bias in enumerate(biases):
            extra = jnp.where(lane == number, bias, extra)
        extra = extra.astype(jnp.bfloat16)
        for kv in range(kv_heads):
            k_buf[kv, pl.ds(start, BLOCK), pl.ds(0, HD)] = split[:BLOCK, kv * HD : (kv + 1) * HD]
            k_buf[kv, pl.ds(start, BLOCK), pl.ds(HD, HD)] = extra
            v_buf[kv, pl.ds(0, HD), pl.ds(start, BLOCK)] = split[BLOCK:, kv * HD : (kv + 1) * HD].T
            v_buf[kv, pl.ds(HD, PAD), pl.ds(start, BLOCK)] = jnp.ones((PAD, BLOCK), jnp.bfloat16)

    lane = lax.broadcasted_iota(jnp.int32, (BLOCK, HD), 1)
    token = lax.broadcasted_iota(jnp.int32, (BLOCK, HD), 0)
    finished_bias = jnp.where(owner_ref[0] == me, 0.0, FLOOR)
    fresh_bias = jnp.where(token < jnp.minimum(valid_ref[0] - me * rows, rows), 0.0, FLOOR)
    full = split_matrix(BLOCK)
    for i in range(pieces):
        local[i].wait()

        def part_cache(step, carry, i=i):
            start = pl.multiple_of(i * piece + step * BLOCK, BLOCK)
            number = i * (piece // BLOCK) + step
            biases = [
                jnp.where(mask_ref[row, number] > 0, 0.0, FLOOR) for row in range(query_blocks)
            ]
            part_block(full, cache_raw[pl.ds(start, BLOCK)], start, biases)
            return carry

        lax.fori_loop(0, piece // BLOCK, part_cache, 0, unroll=4)
    local[pieces].wait()
    for i in range(finished // BLOCK):
        start = context + i * BLOCK
        part_block(full, fin_raw[pl.ds(i * BLOCK, BLOCK)], start, [finished_bias] * query_blocks)
    local[pieces + 1].wait()
    start = context + finished
    part_block(split_matrix(rows), seg_raw[...], start, [fresh_bias] * query_blocks)

    batch = group * rows
    blocks = (context + finished) // BLOCK + 1
    tiles = [range(i, min(i + TILE, blocks)) for i in range(0, blocks, TILE)]
    scale = LOG2E * HD**-0.5
    stat_row = lax.broadcasted_iota(jnp.int32, (PAD, batch), 0)

    def attend(kv, step, carry):
        distance = jnp.where(step < n // 2 + 1, step + n // 2 - 1, step - n // 2)
        distance = jnp.where(step == 0, 0, distance)
        chunk = me ^ distance

        @pl.when(step > 0)
        def _():
            q_copy(kv, chunk, chunk, distance).wait_recv()

        for bit in bits[1:]:

            @pl.when((step > 0) & (distance % (2 * bit) == 0))
            def _():
                q_copy(kv, me ^ bit, chunk, distance + bit).start()

        query_block = (chunk * rows) // BLOCK
        queries = jnp.concatenate(
            [q_buf[kv, chunk, :, pl.ds(g * HD, HD)].astype(jnp.float32) for g in range(group)],
            axis=0,
        ).T
        mark = lax.broadcasted_iota(jnp.int32, (HD, batch), 0) == query_block
        queries = jnp.concatenate([queries, jnp.where(mark, 1.0, 0.0)], axis=0)
        queries = queries.astype(jnp.bfloat16)

        def score_tile(peak, tile):
            start, size = tile[0] * BLOCK, len(tile) * BLOCK
            scores = jnp.dot(
                k_buf[kv, pl.ds(start, size), :], queries, preferred_element_type=jnp.float32
            )
            score_buf[pl.ds(start, size), :] = scores
            return jnp.maximum(peak, jnp.max(scores.reshape(size // 8, 8, batch), axis=0))

        def value_tile(peak, tile):
            start, size = tile[0] * BLOCK, len(tile) * BLOCK
            weights = jnp.exp2((score_buf[pl.ds(start, size), :] - peak) * scale)
            return jnp.dot(
                v_buf[kv, :, pl.ds(start, size)],
                weights.astype(jnp.bfloat16),
                preferred_element_type=jnp.float32,
            )

        def cut(tile):
            return [tile[i : i + SUB] for i in range(0, len(tile), SUB)]

        floor = jnp.full((8, batch), CEIL, jnp.float32)
        ahead = floor
        for part in cut(tiles[0]):
            ahead = score_tile(ahead, part)
        peak, summed = None, None
        for number, tile in enumerate(tiles):
            tile_peak = jnp.max(ahead, axis=0, keepdims=True)
            ahead, later = floor, cut(tiles[number + 1]) if number + 1 < len(tiles) else []
            term = None
            for part in cut(tile):
                if later:
                    ahead = score_tile(ahead, later.pop(0))
                piece_term = value_tile(tile_peak, part)
                term = piece_term if term is None else term + piece_term
            for part in later:
                ahead = score_tile(ahead, part)
            if summed is None:
                peak, summed = tile_peak, term
            else:
                joined = jnp.maximum(peak, tile_peak)
                old, new = jnp.exp2((peak - joined) * scale), jnp.exp2((tile_peak - joined) * scale)
                summed = summed * old + term * new
                peak = joined
        total = summed[HD : HD + 1]
        some = total > 0.0
        safe = jnp.where(some, total, 1.0)
        log_total = jnp.where(some, peak * scale + jnp.log2(safe), FLOOR)
        part_send[kv, chunk, pl.ds(0, HD), :] = (summed[:HD] * (1.0 / safe)).astype(jnp.bfloat16)
        high = log_total.astype(jnp.bfloat16).astype(jnp.float32)
        middle = (log_total - high).astype(jnp.bfloat16).astype(jnp.float32)
        stats = jnp.zeros((PAD, batch), jnp.float32)
        for i, value in enumerate((high, middle, log_total - high - middle)):
            stats = jnp.where(stat_row == i, value, stats)
        part_send[kv, chunk, pl.ds(HD, PAD), :] = stats.astype(jnp.bfloat16)

        @pl.when(keeper(chunk) != me)
        def _():
            part_copy(kv, chunk, me).start()

        if kv > 0:

            @pl.when(step == n // 2)
            def _():
                merge(kv - 1)

        return carry

    def merge(kv):
        @pl.when((me == half - 1) | (me == half))
        def _():
            for slot in range(half):
                merge_slot(kv, me - lax.rem(me, half) + slot, slot)

    def merge_slot(kv, chunk, slot):
        sources = [part_send.at[kv, chunk]]
        for i in order[1:]:
            peer = me ^ i
            part_copy(kv, chunk, peer).wait_recv()
            sources.append(part_recv.at[kv, slot, peer])
        logs = [
            jnp.sum(source[pl.ds(HD, PAD), :].astype(jnp.float32)[:3], axis=0, keepdims=True)
            for source in sources
        ]
        top = functools.reduce(jnp.maximum, logs)
        factors = [jnp.exp2(value - top) for value in logs]
        inverse = 1.0 / functools.reduce(jnp.add, factors)
        terms = [
            source[pl.ds(0, HD), :].astype(jnp.float32) * (factor * inverse)
            for source, factor in zip(sources, factors)
        ]
        merged = functools.reduce(jnp.add, terms).T
        for g in range(group):
            columns = pl.ds(g * HD, HD)
            att_buf[kv, chunk, :, columns] = merged[g * rows : (g + 1) * rows].astype(jnp.bfloat16)
        spread(kv, chunk)

    for kv in range(kv_heads):
        lax.fori_loop(0, n, functools.partial(attend, kv), 0)

    share = n // heads
    last = kv_heads - 1
    arrived = set()

    def collect(kv, distance):
        if (kv, distance) in arrived:
            return
        arrived.add((kv, distance))
        chunk = me ^ distance

        @pl.when(keeper(chunk) != me)
        def _():
            att_copy(kv, chunk, 0).wait_recv()
            spread(kv, chunk)

    def project(kv, i):
        target = (me // share) ^ i
        for j in range(share):
            collect(kv, i * share + j)
        attended = stack_rows([att_buf[kv, target * share + j] for j in range(share)], rows)
        product = jnp.dot(
            attended,
            w_buf[pl.ds(kv * chunk_width, chunk_width), :],
            preferred_element_type=jnp.float32,
        )
        if kv > 0:
            product = product + prod_buf[i]
        if kv < last:
            prod_buf[i] = product
            return

        @pl.when(target == my_head)
        def _():
            out_ref[...] = product

        @pl.when(target != my_head)
        def _():
            proj_send[target] = product.astype(jnp.bfloat16)
            proj_copy(target, my_head).start()

    local[pieces + 2].wait()

    for kv in range(last):
        for distance in range(n - 1, -1, -1):
            collect(kv, distance)
    merge(last)
    for kv in range(kv_heads):
        for i in range(heads):
            project(kv, i)

    for i in range(1, heads):
        peer = lax.rem(my_head + i, heads)
        proj_copy(peer, peer).wait_recv()
        out_ref[...] += proj_recv[peer].astype(jnp.float32)

    for kv in range(kv_heads):
        for i in range(1, n):
            q_copy(kv, me ^ i, me, i).wait_send()
        for chunk in range(n):

            @pl.when(keeper(chunk) != me)
            def _():
                part_copy(kv, chunk, me).wait_send()

            for side, goes in enumerate(att_sides(chunk)):

                @pl.when(goes)
                def _():
                    att_copy(kv, chunk, side).wait_send()

    for i in range(1, heads):
        proj_copy(lax.rem(my_head + i, heads), my_head).wait_send()


def per_device(n, heads, *args):
    query, segment, finished, cache, mask, owner, valid, weight = args
    rows, width = query.shape
    kv_width = segment.shape[2]
    kv_heads = kv_width // HD
    total = cache.shape[0] + finished.shape[0] + BLOCK
    batch = rows * width // kv_width
    out_rows = rows * n // heads
    bf16, f32 = jnp.bfloat16, jnp.float32
    hbm = pl.BlockSpec(memory_space=pl.ANY)
    vmem = pl.BlockSpec(memory_space=pltpu.VMEM)
    smem = pl.BlockSpec(memory_space=pltpu.SMEM)
    dma = pltpu.SemaphoreType.DMA
    return pl.pallas_call(
        functools.partial(kernel, n, heads),
        out_shape=jax.ShapeDtypeStruct((out_rows, weight.shape[1]), f32),
        in_specs=[vmem, hbm, hbm, hbm, smem, smem, smem, hbm],
        out_specs=vmem,
        scratch_shapes=[
            pltpu.VMEM(cache.shape, bf16),
            pltpu.VMEM(finished.shape, bf16),
            pltpu.VMEM(segment.shape, bf16),
            pltpu.VMEM(weight.shape, bf16),
            pltpu.VMEM((kv_heads, total, 2 * HD), bf16),
            pltpu.VMEM((kv_heads, HD + PAD, total), bf16),
            pltpu.VMEM((total, batch), f32),
            pltpu.VMEM((kv_heads, n, rows, width // kv_heads), bf16),
            pltpu.VMEM((kv_heads, n, HD + PAD, batch), bf16),
            pltpu.VMEM((kv_heads, n // 2, n, HD + PAD, batch), bf16),
            pltpu.VMEM((kv_heads, n, rows, width // kv_heads), bf16),
            pltpu.VMEM((heads, out_rows, weight.shape[1]), f32),
            pltpu.VMEM((heads, out_rows, weight.shape[1]), bf16),
            pltpu.VMEM((heads, out_rows, weight.shape[1]), bf16),
            dma((7,)),
            dma((kv_heads, n)),
            dma((kv_heads, n)),
            dma((kv_heads, n)),
            dma((kv_heads, n // 2, n)),
            dma((2, kv_heads, n)),
            dma((kv_heads, n)),
            dma((heads,)),
            dma((heads,)),
        ],
        compiler_params=pltpu.CompilerParams(
            collective_id=0, has_side_effects=True, vmem_limit_bytes=56 << 20
        ),
    )(query, segment, finished, cache, mask, owner, valid, weight)


def solution(mesh):
    return jax.shard_map(
        functools.partial(per_device, mesh.shape["seq"], mesh.shape["head"]),
        mesh=mesh,
        in_specs=(
            P(("groups", "seq"), "head"),
            P(("groups", "seq"), None, "head"),
            P(("groups", "seq"), None, "head"),
            P(("groups", "seq"), None, "head"),
            P("groups", "seq"),
            P("groups"),
            P("groups"),
            P("head", "seq"),
        ),
        out_specs=P(("groups", "head"), "seq"),
        check_vma=False,
    )
```

```python
import functools

import jax
import jax.numpy as jnp
from jax import lax
from jax.experimental import pallas as pl
from jax.experimental.pallas import tpu as pltpu
from jax.sharding import PartitionSpec as P

HD = 128
BLOCK = 128
TILE = 8
SUB = 2
PAD = 16
FLOOR = -1e30
CEIL = -1e29
LOG2E = 1.4426950408889634


def split_matrix(tokens):
    row = lax.broadcasted_iota(jnp.int32, (2 * BLOCK, 2 * tokens), 0)
    col = lax.broadcasted_iota(jnp.int32, (2 * BLOCK, 2 * tokens), 1)
    want = jnp.where(row < BLOCK, 2 * row, 2 * (row - BLOCK) + 1)
    return jnp.where(row % BLOCK < tokens, jnp.where(col == want, 1.0, 0.0), 0.0).astype(jnp.bfloat16)


def stack_rows(pieces, rows):
    if rows % 16 == 0:
        return jnp.concatenate(pieces, axis=0)
    wide = [piece.astype(jnp.float32) for piece in pieces]
    return jnp.concatenate(wide, axis=0).astype(jnp.bfloat16)


def kernel(
    n,
    heads,
    q_ref,
    seg_hbm,
    fin_hbm,
    cache_hbm,
    mask_ref,
    owner_ref,
    valid_ref,
    w_hbm,
    out_ref,
    cache_raw,
    fin_raw,
    seg_raw,
    w_buf,
    k_buf,
    v_buf,
    score_buf,
    q_buf,
    part_send,
    part_recv,
    att_buf,
    prod_buf,
    proj_send,
    proj_recv,
    local_sem,
    q_send_sem,
    q_recv_sem,
    part_send_sem,
    part_recv_sem,
    att_send_sem,
    att_recv_sem,
    proj_send_sem,
    proj_recv_sem,
):
    me = lax.axis_index("seq")
    my_head = lax.axis_index("head")
    rows, width = q_ref.shape
    kv_heads = k_buf.shape[0]
    query_blocks = mask_ref.shape[0]
    group = width // (kv_heads * HD)
    context = cache_raw.shape[0]
    finished = fin_raw.shape[0]
    order = [0, *range(n // 2, n), *range(1, n // 2)]
    pieces = 4
    piece = context // pieces

    local = [
        pltpu.make_async_copy(
            cache_hbm.at[pl.ds(i * piece, piece)],
            cache_raw.at[pl.ds(i * piece, piece)],
            local_sem.at[i],
        )
        for i in range(pieces)
    ]
    local.append(pltpu.make_async_copy(fin_hbm, fin_raw, local_sem.at[pieces]))
    local.append(pltpu.make_async_copy(seg_hbm, seg_raw, local_sem.at[pieces + 1]))
    local.append(pltpu.make_async_copy(w_hbm, w_buf, local_sem.at[pieces + 2]))
    for copy in local:
        copy.start()

    chunk_width = width // kv_heads
    for kv in range(kv_heads):
        q_buf[kv, me] = q_ref[:, pl.ds(kv * chunk_width, chunk_width)]

    barrier = pltpu.get_barrier_semaphore()
    for i in range(1, n):
        pl.semaphore_signal(barrier, inc=1, device_id={"seq": lax.rem(me + i, n)})
    for i in range(1, heads):
        pl.semaphore_signal(barrier, inc=1, device_id={"head": lax.rem(my_head + i, heads)})
    pl.semaphore_wait(barrier, n + heads - 2)

    def seq_copy(source, target_buf, sems, kv, mark, target, owner):
        return pltpu.make_async_remote_copy(
            src_ref=source,
            dst_ref=target_buf.at[kv, owner],
            send_sem=sems[0].at[kv, mark],
            recv_sem=sems[1].at[kv, owner],
            device_id={"seq": target},
        )

    def q_copy(kv, target, owner, mark):
        sems = (q_send_sem, q_recv_sem)
        return seq_copy(q_buf.at[kv, owner], q_buf, sems, kv, mark, target, owner)

    def part_copy(kv, target, owner, mark):
        sems = (part_send_sem, part_recv_sem)
        return seq_copy(part_send.at[kv, target], part_recv, sems, kv, mark, target, owner)

    def att_copy(kv, target, owner, mark):
        sems = (att_send_sem, att_recv_sem)
        return seq_copy(att_buf.at[kv, owner], att_buf, sems, kv, mark, target, owner)

    def proj_copy(target, owner):
        return pltpu.make_async_remote_copy(
            src_ref=proj_send.at[target],
            dst_ref=proj_recv.at[owner],
            send_sem=proj_send_sem.at[target],
            recv_sem=proj_recv_sem.at[owner],
            device_id={"head": target},
        )

    bits = [n >> (i + 1) for i in range(n.bit_length() - 1)]
    for kv in range(kv_heads):
        for bit in bits:
            q_copy(kv, me ^ bit, me, bit).start()

    def part_block(matrix, raw, start, biases):
        pair = raw.reshape(2 * raw.shape[0], raw.shape[2])
        split = jnp.dot(matrix, pair, preferred_element_type=jnp.float32).astype(jnp.bfloat16)
        extra = jnp.zeros((BLOCK, HD), jnp.float32)
        for number, bias in enumerate(biases):
            extra = jnp.where(lane == number, bias, extra)
        extra = extra.astype(jnp.bfloat16)
        for kv in range(kv_heads):
            k_buf[kv, pl.ds(start, BLOCK), pl.ds(0, HD)] = split[:BLOCK, kv * HD : (kv + 1) * HD]
            k_buf[kv, pl.ds(start, BLOCK), pl.ds(HD, HD)] = extra
            v_buf[kv, pl.ds(0, HD), pl.ds(start, BLOCK)] = split[BLOCK:, kv * HD : (kv + 1) * HD].T
            v_buf[kv, pl.ds(HD, PAD), pl.ds(start, BLOCK)] = jnp.ones((PAD, BLOCK), jnp.bfloat16)

    lane = lax.broadcasted_iota(jnp.int32, (BLOCK, HD), 1)
    token = lax.broadcasted_iota(jnp.int32, (BLOCK, HD), 0)
    finished_bias = jnp.where(owner_ref[0] == me, 0.0, FLOOR)
    fresh_bias = jnp.where(token < jnp.minimum(valid_ref[0] - me * rows, rows), 0.0, FLOOR)
    full = split_matrix(BLOCK)
    for i in range(pieces):
        local[i].wait()

        def part_cache(step, carry, i=i):
            start = pl.multiple_of(i * piece + step * BLOCK, BLOCK)
            number = i * (piece // BLOCK) + step
            biases = [
                jnp.where(mask_ref[row, number] > 0, 0.0, FLOOR) for row in range(query_blocks)
            ]
            part_block(full, cache_raw[pl.ds(start, BLOCK)], start, biases)
            return carry

        lax.fori_loop(0, piece // BLOCK, part_cache, 0, unroll=4)
    local[pieces].wait()
    for i in range(finished // BLOCK):
        start = context + i * BLOCK
        part_block(full, fin_raw[pl.ds(i * BLOCK, BLOCK)], start, [finished_bias] * query_blocks)
    local[pieces + 1].wait()
    start = context + finished
    part_block(split_matrix(rows), seg_raw[...], start, [fresh_bias] * query_blocks)

    batch = group * rows
    blocks = (context + finished) // BLOCK + 1
    tiles = [range(i, min(i + TILE, blocks)) for i in range(0, blocks, TILE)]
    scale = LOG2E * HD**-0.5
    stat_row = lax.broadcasted_iota(jnp.int32, (PAD, batch), 0)

    def attend(kv, step, carry):
        distance = jnp.where(step < n // 2 + 1, step + n // 2 - 1, step - n // 2)
        distance = jnp.where(step == 0, 0, distance)
        chunk = me ^ distance

        @pl.when(step > 0)
        def _():
            q_copy(kv, chunk, chunk, distance).wait_recv()

        for bit in bits[1:]:

            @pl.when((step > 0) & (distance % (2 * bit) == 0))
            def _():
                q_copy(kv, me ^ bit, chunk, distance + bit).start()

        query_block = (chunk * rows) // BLOCK
        queries = jnp.concatenate(
            [q_buf[kv, chunk, :, pl.ds(g * HD, HD)].astype(jnp.float32) for g in range(group)],
            axis=0,
        ).T
        mark = lax.broadcasted_iota(jnp.int32, (HD, batch), 0) == query_block
        queries = jnp.concatenate([queries, jnp.where(mark, 1.0, 0.0)], axis=0)
        queries = queries.astype(jnp.bfloat16)

        def score_tile(peak, tile):
            start, size = tile[0] * BLOCK, len(tile) * BLOCK
            scores = jnp.dot(
                k_buf[kv, pl.ds(start, size), :], queries, preferred_element_type=jnp.float32
            )
            score_buf[pl.ds(start, size), :] = scores
            return jnp.maximum(peak, jnp.max(scores.reshape(size // 8, 8, batch), axis=0))

        def value_tile(peak, tile):
            start, size = tile[0] * BLOCK, len(tile) * BLOCK
            weights = jnp.exp2((score_buf[pl.ds(start, size), :] - peak) * scale)
            return jnp.dot(
                v_buf[kv, :, pl.ds(start, size)],
                weights.astype(jnp.bfloat16),
                preferred_element_type=jnp.float32,
            )

        def cut(tile):
            return [tile[i : i + SUB] for i in range(0, len(tile), SUB)]

        floor = jnp.full((8, batch), CEIL, jnp.float32)
        ahead = floor
        for part in cut(tiles[0]):
            ahead = score_tile(ahead, part)
        peak, summed = None, None
        for number, tile in enumerate(tiles):
            tile_peak = jnp.max(ahead, axis=0, keepdims=True)
            ahead, later = floor, cut(tiles[number + 1]) if number + 1 < len(tiles) else []
            term = None
            for part in cut(tile):
                if later:
                    ahead = score_tile(ahead, later.pop(0))
                piece_term = value_tile(tile_peak, part)
                term = piece_term if term is None else term + piece_term
            for part in later:
                ahead = score_tile(ahead, part)
            if summed is None:
                peak, summed = tile_peak, term
            else:
                joined = jnp.maximum(peak, tile_peak)
                old, new = jnp.exp2((peak - joined) * scale), jnp.exp2((tile_peak - joined) * scale)
                summed = summed * old + term * new
                peak = joined
        total = summed[HD : HD + 1]
        some = total > 0.0
        safe = jnp.where(some, total, 1.0)
        log_total = jnp.where(some, peak * scale + jnp.log2(safe), FLOOR)
        part_send[kv, chunk, pl.ds(0, HD), :] = (summed[:HD] * (1.0 / safe)).astype(jnp.bfloat16)
        high = log_total.astype(jnp.bfloat16).astype(jnp.float32)
        middle = (log_total - high).astype(jnp.bfloat16).astype(jnp.float32)
        stats = jnp.zeros((PAD, batch), jnp.float32)
        for i, value in enumerate((high, middle, log_total - high - middle)):
            stats = jnp.where(stat_row == i, value, stats)
        part_send[kv, chunk, pl.ds(HD, PAD), :] = stats.astype(jnp.bfloat16)

        @pl.when(step > 0)
        def _():
            part_copy(kv, chunk, me, distance).start()

        if kv > 0:

            @pl.when(step == n // 2)
            def _():
                merge(kv - 1)

        return carry

    def spread(kv, distance):
        step = (distance & -distance if distance else n) // 2
        while step:
            att_copy(kv, me ^ step, me ^ distance, distance + step).start()
            step //= 2

    def merge(kv):
        sources = [part_send.at[kv, me]]
        for i in order[1:]:
            peer = me ^ i
            part_copy(kv, peer, peer, i).wait_recv()
            sources.append(part_recv.at[kv, peer])
        logs = [
            jnp.sum(source[pl.ds(HD, PAD), :].astype(jnp.float32)[:3], axis=0, keepdims=True)
            for source in sources
        ]
        top = functools.reduce(jnp.maximum, logs)
        factors = [jnp.exp2(value - top) for value in logs]
        inverse = 1.0 / functools.reduce(jnp.add, factors)
        terms = [
            source[pl.ds(0, HD), :].astype(jnp.float32) * (factor * inverse)
            for source, factor in zip(sources, factors)
        ]
        merged = functools.reduce(jnp.add, terms).T
        for g in range(group):
            columns = pl.ds(g * HD, HD)
            att_buf[kv, me, :, columns] = merged[g * rows : (g + 1) * rows].astype(jnp.bfloat16)
        spread(kv, 0)

    for kv in range(kv_heads):
        lax.fori_loop(0, n, functools.partial(attend, kv), 0)

    share = n // heads
    last = kv_heads - 1
    arrived = set()

    def collect(kv, distance):
        if distance and (kv, distance) not in arrived:
            arrived.add((kv, distance))
            att_copy(kv, me ^ distance, me ^ distance, distance).wait_recv()
            spread(kv, distance)

    def collect_all(kv):
        for distance in sorted(range(1, n), key=lambda d: (d.bit_count(), -d)):
            collect(kv, distance)

    def project_early():
        out_rows = out_ref.shape[0]
        for kv in range(last):
            collect_all(kv)
            flat = stack_rows([att_buf[kv, j] for j in range(n)], rows)
            product = jnp.dot(
                flat,
                w_buf[pl.ds(kv * chunk_width, chunk_width), :],
                preferred_element_type=jnp.float32,
            )
            for i in range(heads):
                part = product[i * out_rows : (i + 1) * out_rows]
                prod_buf[i] = part if kv == 0 else prod_buf[i] + part

    def project(kv, i):
        target = (me // share) ^ i
        if share == 1:
            collect(kv, i)
        else:
            collect_all(kv)
        attended = stack_rows([att_buf[kv, target * share + j] for j in range(share)], rows)
        product = jnp.dot(
            attended,
            w_buf[pl.ds(kv * chunk_width, chunk_width), :],
            preferred_element_type=jnp.float32,
        )
        if last > 0:
            product = product + prod_buf[target]

        @pl.when(target == my_head)
        def _():
            out_ref[...] = product

        @pl.when(target != my_head)
        def _():
            proj_send[target] = product.astype(jnp.bfloat16)
            proj_copy(target, my_head).start()

    local[pieces + 2].wait()

    head_order = [0] + sorted(range(1, heads), key=lambda d: (d.bit_count(), -d))
    for kv in range(last):
        collect(kv, n // 2)
    merge(last)
    project_early()
    for i in head_order:
        project(last, i)

    for i in range(1, heads):
        peer = lax.rem(my_head + i, heads)
        proj_copy(peer, peer).wait_recv()
        out_ref[...] += proj_recv[peer].astype(jnp.float32)

    for kv in range(kv_heads):
        for i in range(1, n):
            q_copy(kv, me ^ i, me, i).wait_send()
            part_copy(kv, me ^ i, me, i).wait_send()
            att_copy(kv, me ^ i, me, i).wait_send()
    for i in range(1, heads):
        proj_copy(lax.rem(my_head + i, heads), my_head).wait_send()


def per_device(n, heads, *args):
    query, segment, finished, cache, mask, owner, valid, weight = args
    rows, width = query.shape
    kv_width = segment.shape[2]
    kv_heads = kv_width // HD
    total = cache.shape[0] + finished.shape[0] + BLOCK
    batch = rows * width // kv_width
    out_rows = rows * n // heads
    bf16, f32 = jnp.bfloat16, jnp.float32
    hbm = pl.BlockSpec(memory_space=pl.ANY)
    vmem = pl.BlockSpec(memory_space=pltpu.VMEM)
    smem = pl.BlockSpec(memory_space=pltpu.SMEM)
    dma = pltpu.SemaphoreType.DMA
    return pl.pallas_call(
        functools.partial(kernel, n, heads),
        out_shape=jax.ShapeDtypeStruct((out_rows, weight.shape[1]), f32),
        in_specs=[vmem, hbm, hbm, hbm, smem, smem, smem, hbm],
        out_specs=vmem,
        scratch_shapes=[
            pltpu.VMEM(cache.shape, bf16),
            pltpu.VMEM(finished.shape, bf16),
            pltpu.VMEM(segment.shape, bf16),
            pltpu.VMEM(weight.shape, bf16),
            pltpu.VMEM((kv_heads, total, 2 * HD), bf16),
            pltpu.VMEM((kv_heads, HD + PAD, total), bf16),
            pltpu.VMEM((total, batch), f32),
            pltpu.VMEM((kv_heads, n, rows, width // kv_heads), bf16),
            pltpu.VMEM((kv_heads, n, HD + PAD, batch), bf16),
            pltpu.VMEM((kv_heads, n, HD + PAD, batch), bf16),
            pltpu.VMEM((kv_heads, n, rows, width // kv_heads), bf16),
            pltpu.VMEM((heads, out_rows, weight.shape[1]), f32),
            pltpu.VMEM((heads, out_rows, weight.shape[1]), bf16),
            pltpu.VMEM((heads, out_rows, weight.shape[1]), bf16),
            dma((7,)),
            dma((kv_heads, n)),
            dma((kv_heads, n)),
            dma((kv_heads, n)),
            dma((kv_heads, n)),
            dma((kv_heads, n)),
            dma((kv_heads, n)),
            dma((heads,)),
            dma((heads,)),
        ],
        compiler_params=pltpu.CompilerParams(
            collective_id=0, has_side_effects=True, vmem_limit_bytes=56 << 20
        ),
    )(query, segment, finished, cache, mask, owner, valid, weight)


def solution(mesh):
    return jax.shard_map(
        functools.partial(per_device, mesh.shape["seq"], mesh.shape["head"]),
        mesh=mesh,
        in_specs=(
            P(("groups", "seq"), "head"),
            P(("groups", "seq"), None, "head"),
            P(("groups", "seq"), None, "head"),
            P(("groups", "seq"), None, "head"),
            P("groups", "seq"),
            P("groups"),
            P("groups"),
            P("head", "seq"),
        ),
        out_specs=P(("groups", "head"), "seq"),
        check_vma=False,
    )
```

```python
import functools

import jax
import jax.numpy as jnp
from jax import lax
from jax.experimental import pallas as pl
from jax.experimental.pallas import tpu as pltpu
from jax.sharding import PartitionSpec as P

HD = 128
BLOCK = 128
TILE = 8
SUB = 2
PAD = 16
FLOOR = -1e30
CEIL = -1e29
LOG2E = 1.4426950408889634


def split_matrix(tokens):
    row = lax.broadcasted_iota(jnp.int32, (2 * BLOCK, 2 * tokens), 0)
    col = lax.broadcasted_iota(jnp.int32, (2 * BLOCK, 2 * tokens), 1)
    want = jnp.where(row < BLOCK, 2 * row, 2 * (row - BLOCK) + 1)
    return jnp.where(row % BLOCK < tokens, jnp.where(col == want, 1.0, 0.0), 0.0).astype(jnp.bfloat16)


def stack_rows(pieces, rows):
    if rows % 16 == 0:
        return jnp.concatenate(pieces, axis=0)
    wide = [piece.astype(jnp.float32) for piece in pieces]
    return jnp.concatenate(wide, axis=0).astype(jnp.bfloat16)


def kernel(
    n,
    heads,
    q_ref,
    seg_hbm,
    fin_hbm,
    cache_hbm,
    mask_ref,
    owner_ref,
    valid_ref,
    w_hbm,
    out_ref,
    cache_raw,
    fin_raw,
    seg_raw,
    w_buf,
    k_buf,
    v_buf,
    score_buf,
    q_buf,
    part_send,
    part_recv,
    att_buf,
    prod_buf,
    proj_send,
    proj_recv,
    local_sem,
    q_send_sem,
    q_recv_sem,
    part_send_sem,
    part_recv_sem,
    att_send_sem,
    att_recv_sem,
    proj_send_sem,
    proj_recv_sem,
):
    me = lax.axis_index("seq")
    my_head = lax.axis_index("head")
    rows, width = q_ref.shape
    kv_heads = k_buf.shape[0]
    query_blocks = mask_ref.shape[0]
    group = width // (kv_heads * HD)
    context = cache_raw.shape[0]
    finished = fin_raw.shape[0]
    order = [0, *range(n // 2, n), *range(1, n // 2)]
    pieces = 4
    piece = context // pieces

    local = [
        pltpu.make_async_copy(
            cache_hbm.at[pl.ds(i * piece, piece)],
            cache_raw.at[pl.ds(i * piece, piece)],
            local_sem.at[i],
        )
        for i in range(pieces)
    ]
    local.append(pltpu.make_async_copy(fin_hbm, fin_raw, local_sem.at[pieces]))
    local.append(pltpu.make_async_copy(seg_hbm, seg_raw, local_sem.at[pieces + 1]))
    local.append(pltpu.make_async_copy(w_hbm, w_buf, local_sem.at[pieces + 2]))
    for copy in local:
        copy.start()

    chunk_width = width // kv_heads
    for kv in range(kv_heads):
        q_buf[kv, me] = q_ref[:, pl.ds(kv * chunk_width, chunk_width)]

    barrier = pltpu.get_barrier_semaphore()
    for i in range(1, n):
        pl.semaphore_signal(barrier, inc=1, device_id={"seq": lax.rem(me + i, n)})
    for i in range(1, heads):
        pl.semaphore_signal(barrier, inc=1, device_id={"head": lax.rem(my_head + i, heads)})
    pl.semaphore_wait(barrier, n + heads - 2)

    def seq_copy(source, target_buf, sems, kv, mark, target, owner):
        return pltpu.make_async_remote_copy(
            src_ref=source,
            dst_ref=target_buf.at[kv, owner],
            send_sem=sems[0].at[kv, mark],
            recv_sem=sems[1].at[kv, owner],
            device_id={"seq": target},
        )

    def q_copy(kv, target, owner, mark):
        sems = (q_send_sem, q_recv_sem)
        return seq_copy(q_buf.at[kv, owner], q_buf, sems, kv, mark, target, owner)

    def part_copy(kv, target, owner, mark):
        sems = (part_send_sem, part_recv_sem)
        return seq_copy(part_send.at[kv, target], part_recv, sems, kv, mark, target, owner)

    def att_copy(kv, target, owner, mark):
        sems = (att_send_sem, att_recv_sem)
        return seq_copy(att_buf.at[kv, owner], att_buf, sems, kv, mark, target, owner)

    def proj_copy(target, owner):
        return pltpu.make_async_remote_copy(
            src_ref=proj_send.at[target],
            dst_ref=proj_recv.at[owner],
            send_sem=proj_send_sem.at[target],
            recv_sem=proj_recv_sem.at[owner],
            device_id={"head": target},
        )

    bits = [n >> (i + 1) for i in range(n.bit_length() - 1)]
    for kv in range(kv_heads):
        for bit in bits:
            q_copy(kv, me ^ bit, me, bit).start()

    def part_block(matrix, raw, start, biases):
        pair = raw.reshape(2 * raw.shape[0], raw.shape[2])
        split = jnp.dot(matrix, pair, preferred_element_type=jnp.float32).astype(jnp.bfloat16)
        extra = jnp.zeros((BLOCK, HD), jnp.float32)
        for number, bias in enumerate(biases):
            extra = jnp.where(lane == number, bias, extra)
        extra = extra.astype(jnp.bfloat16)
        for kv in range(kv_heads):
            k_buf[kv, pl.ds(start, BLOCK), pl.ds(0, HD)] = split[:BLOCK, kv * HD : (kv + 1) * HD]
            k_buf[kv, pl.ds(start, BLOCK), pl.ds(HD, HD)] = extra
            v_buf[kv, pl.ds(0, HD), pl.ds(start, BLOCK)] = split[BLOCK:, kv * HD : (kv + 1) * HD].T
            v_buf[kv, pl.ds(HD, PAD), pl.ds(start, BLOCK)] = jnp.ones((PAD, BLOCK), jnp.bfloat16)

    lane = lax.broadcasted_iota(jnp.int32, (BLOCK, HD), 1)
    token = lax.broadcasted_iota(jnp.int32, (BLOCK, HD), 0)
    finished_bias = jnp.where(owner_ref[0] == me, 0.0, FLOOR)
    fresh_bias = jnp.where(token < jnp.minimum(valid_ref[0] - me * rows, rows), 0.0, FLOOR)
    full = split_matrix(BLOCK)
    for i in range(pieces):
        local[i].wait()

        def part_cache(step, carry, i=i):
            start = pl.multiple_of(i * piece + step * BLOCK, BLOCK)
            number = i * (piece // BLOCK) + step
            biases = [
                jnp.where(mask_ref[row, number] > 0, 0.0, FLOOR) for row in range(query_blocks)
            ]
            part_block(full, cache_raw[pl.ds(start, BLOCK)], start, biases)
            return carry

        lax.fori_loop(0, piece // BLOCK, part_cache, 0, unroll=4)
    local[pieces].wait()
    for i in range(finished // BLOCK):
        start = context + i * BLOCK
        part_block(full, fin_raw[pl.ds(i * BLOCK, BLOCK)], start, [finished_bias] * query_blocks)
    local[pieces + 1].wait()
    start = context + finished
    part_block(split_matrix(rows), seg_raw[...], start, [fresh_bias] * query_blocks)

    batch = group * rows
    blocks = (context + finished) // BLOCK + 1
    tiles = [range(i, min(i + TILE, blocks)) for i in range(0, blocks, TILE)]
    scale = LOG2E * HD**-0.5
    stat_row = lax.broadcasted_iota(jnp.int32, (PAD, batch), 0)

    def attend(kv, turn, carry):
        step = turn if kv == 0 else lax.rem(turn + 1, n)
        distance = jnp.where(step < n // 2 + 1, step + n // 2 - 1, step - n // 2)
        distance = jnp.where(step == 0, 0, distance)
        chunk = me ^ distance

        @pl.when(step > 0)
        def _():
            q_copy(kv, chunk, chunk, distance).wait_recv()

        for bit in bits[1:]:

            @pl.when((step > 0) & (distance % (2 * bit) == 0))
            def _():
                q_copy(kv, me ^ bit, chunk, distance + bit).start()

        query_block = (chunk * rows) // BLOCK
        queries = jnp.concatenate(
            [q_buf[kv, chunk, :, pl.ds(g * HD, HD)].astype(jnp.float32) for g in range(group)],
            axis=0,
        ).T
        mark = lax.broadcasted_iota(jnp.int32, (HD, batch), 0) == query_block
        queries = jnp.concatenate([queries, jnp.where(mark, 1.0, 0.0)], axis=0)
        queries = queries.astype(jnp.bfloat16)

        def score_tile(peak, tile):
            start, size = tile[0] * BLOCK, len(tile) * BLOCK
            scores = jnp.dot(
                k_buf[kv, pl.ds(start, size), :], queries, preferred_element_type=jnp.float32
            )
            score_buf[pl.ds(start, size), :] = scores
            return jnp.maximum(peak, jnp.max(scores.reshape(size // 8, 8, batch), axis=0))

        def value_tile(peak, tile):
            start, size = tile[0] * BLOCK, len(tile) * BLOCK
            weights = jnp.exp2((score_buf[pl.ds(start, size), :] - peak) * scale)
            return jnp.dot(
                v_buf[kv, :, pl.ds(start, size)],
                weights.astype(jnp.bfloat16),
                preferred_element_type=jnp.float32,
            )

        def cut(tile):
            return [tile[i : i + SUB] for i in range(0, len(tile), SUB)]

        floor = jnp.full((8, batch), CEIL, jnp.float32)
        ahead = floor
        for part in cut(tiles[0]):
            ahead = score_tile(ahead, part)
        peak, summed = None, None
        for number, tile in enumerate(tiles):
            tile_peak = jnp.max(ahead, axis=0, keepdims=True)
            ahead, later = floor, cut(tiles[number + 1]) if number + 1 < len(tiles) else []
            term = None
            for part in cut(tile):
                if later:
                    ahead = score_tile(ahead, later.pop(0))
                piece_term = value_tile(tile_peak, part)
                term = piece_term if term is None else term + piece_term
            for part in later:
                ahead = score_tile(ahead, part)
            if summed is None:
                peak, summed = tile_peak, term
            else:
                joined = jnp.maximum(peak, tile_peak)
                old, new = jnp.exp2((peak - joined) * scale), jnp.exp2((tile_peak - joined) * scale)
                summed = summed * old + term * new
                peak = joined
        total = summed[HD : HD + 1]
        some = total > 0.0
        safe = jnp.where(some, total, 1.0)
        log_total = jnp.where(some, peak * scale + jnp.log2(safe), FLOOR)
        part_send[kv, chunk, pl.ds(0, HD), :] = (summed[:HD] * (1.0 / safe)).astype(jnp.bfloat16)
        high = log_total.astype(jnp.bfloat16).astype(jnp.float32)
        middle = (log_total - high).astype(jnp.bfloat16).astype(jnp.float32)
        stats = jnp.zeros((PAD, batch), jnp.float32)
        for i, value in enumerate((high, middle, log_total - high - middle)):
            stats = jnp.where(stat_row == i, value, stats)
        part_send[kv, chunk, pl.ds(HD, PAD), :] = stats.astype(jnp.bfloat16)

        @pl.when(step > 0)
        def _():
            part_copy(kv, chunk, me, distance).start()

        if kv > 0:

            @pl.when(turn == n // 2)
            def _():
                merge(kv - 1)

        return carry

    def spread(kv, distance):
        step = (distance & -distance if distance else n) // 2
        while step:
            att_copy(kv, me ^ step, me ^ distance, distance + step).start()
            step //= 2

    def merge(kv):
        sources = [part_send.at[kv, me]]
        for i in order[1:]:
            peer = me ^ i
            part_copy(kv, peer, peer, i).wait_recv()
            sources.append(part_recv.at[kv, peer])
        logs = [
            jnp.sum(source[pl.ds(HD, PAD), :].astype(jnp.float32)[:3], axis=0, keepdims=True)
            for source in sources
        ]
        top = functools.reduce(jnp.maximum, logs)
        factors = [jnp.exp2(value - top) for value in logs]
        inverse = 1.0 / functools.reduce(jnp.add, factors)
        terms = [
            source[pl.ds(0, HD), :].astype(jnp.float32) * (factor * inverse)
            for source, factor in zip(sources, factors)
        ]
        merged = functools.reduce(jnp.add, terms).T
        for g in range(group):
            columns = pl.ds(g * HD, HD)
            att_buf[kv, me, :, columns] = merged[g * rows : (g + 1) * rows].astype(jnp.bfloat16)
        spread(kv, 0)

    for kv in range(kv_heads):
        lax.fori_loop(0, n, functools.partial(attend, kv), 0)

    share = n // heads
    last = kv_heads - 1
    arrived = set()

    def collect(kv, distance):
        if distance and (kv, distance) not in arrived:
            arrived.add((kv, distance))
            att_copy(kv, me ^ distance, me ^ distance, distance).wait_recv()
            spread(kv, distance)

    def collect_all(kv):
        for distance in sorted(range(1, n), key=lambda d: (d.bit_count(), -d)):
            collect(kv, distance)

    def project_early():
        out_rows = out_ref.shape[0]
        for kv in range(last):
            collect_all(kv)
            flat = stack_rows([att_buf[kv, j] for j in range(n)], rows)
            product = jnp.dot(
                flat,
                w_buf[pl.ds(kv * chunk_width, chunk_width), :],
                preferred_element_type=jnp.float32,
            )
            for i in range(heads):
                part = product[i * out_rows : (i + 1) * out_rows]
                prod_buf[i] = part if kv == 0 else prod_buf[i] + part

    def project(kv, i):
        target = (me // share) ^ i
        if share == 1:
            collect(kv, i)
        else:
            collect_all(kv)
        attended = stack_rows([att_buf[kv, target * share + j] for j in range(share)], rows)
        product = jnp.dot(
            attended,
            w_buf[pl.ds(kv * chunk_width, chunk_width), :],
            preferred_element_type=jnp.float32,
        )
        if last > 0:
            product = product + prod_buf[target]

        @pl.when(target == my_head)
        def _():
            out_ref[...] = product

        @pl.when(target != my_head)
        def _():
            proj_send[target] = product.astype(jnp.bfloat16)
            proj_copy(target, my_head).start()

    local[pieces + 2].wait()

    head_order = [0] + sorted(range(1, heads), key=lambda d: (d.bit_count(), -d))
    for kv in range(last):
        collect(kv, n // 2)
    merge(last)
    project_early()
    for i in head_order:
        project(last, i)

    for i in range(1, heads):
        peer = lax.rem(my_head + i, heads)
        proj_copy(peer, peer).wait_recv()
        out_ref[...] += proj_recv[peer].astype(jnp.float32)

    for kv in range(kv_heads):
        for i in range(1, n):
            q_copy(kv, me ^ i, me, i).wait_send()
            part_copy(kv, me ^ i, me, i).wait_send()
            att_copy(kv, me ^ i, me, i).wait_send()
    for i in range(1, heads):
        proj_copy(lax.rem(my_head + i, heads), my_head).wait_send()


def per_device(n, heads, *args):
    query, segment, finished, cache, mask, owner, valid, weight = args
    rows, width = query.shape
    kv_width = segment.shape[2]
    kv_heads = kv_width // HD
    total = cache.shape[0] + finished.shape[0] + BLOCK
    batch = rows * width // kv_width
    out_rows = rows * n // heads
    bf16, f32 = jnp.bfloat16, jnp.float32
    hbm = pl.BlockSpec(memory_space=pl.ANY)
    vmem = pl.BlockSpec(memory_space=pltpu.VMEM)
    smem = pl.BlockSpec(memory_space=pltpu.SMEM)
    dma = pltpu.SemaphoreType.DMA
    return pl.pallas_call(
        functools.partial(kernel, n, heads),
        out_shape=jax.ShapeDtypeStruct((out_rows, weight.shape[1]), f32),
        in_specs=[vmem, hbm, hbm, hbm, smem, smem, smem, hbm],
        out_specs=vmem,
        scratch_shapes=[
            pltpu.VMEM(cache.shape, bf16),
            pltpu.VMEM(finished.shape, bf16),
            pltpu.VMEM(segment.shape, bf16),
            pltpu.VMEM(weight.shape, bf16),
            pltpu.VMEM((kv_heads, total, 2 * HD), bf16),
            pltpu.VMEM((kv_heads, HD + PAD, total), bf16),
            pltpu.VMEM((total, batch), f32),
            pltpu.VMEM((kv_heads, n, rows, width // kv_heads), bf16),
            pltpu.VMEM((kv_heads, n, HD + PAD, batch), bf16),
            pltpu.VMEM((kv_heads, n, HD + PAD, batch), bf16),
            pltpu.VMEM((kv_heads, n, rows, width // kv_heads), bf16),
            pltpu.VMEM((heads, out_rows, weight.shape[1]), f32),
            pltpu.VMEM((heads, out_rows, weight.shape[1]), bf16),
            pltpu.VMEM((heads, out_rows, weight.shape[1]), bf16),
            dma((7,)),
            dma((kv_heads, n)),
            dma((kv_heads, n)),
            dma((kv_heads, n)),
            dma((kv_heads, n)),
            dma((kv_heads, n)),
            dma((kv_heads, n)),
            dma((heads,)),
            dma((heads,)),
        ],
        compiler_params=pltpu.CompilerParams(
            collective_id=0, has_side_effects=True, vmem_limit_bytes=56 << 20
        ),
    )(query, segment, finished, cache, mask, owner, valid, weight)


def solution(mesh):
    return jax.shard_map(
        functools.partial(per_device, mesh.shape["seq"], mesh.shape["head"]),
        mesh=mesh,
        in_specs=(
            P(("groups", "seq"), "head"),
            P(("groups", "seq"), None, "head"),
            P(("groups", "seq"), None, "head"),
            P(("groups", "seq"), None, "head"),
            P("groups", "seq"),
            P("groups"),
            P("groups"),
            P("head", "seq"),
        ),
        out_specs=P(("groups", "head"), "seq"),
        check_vma=False,
    )
```
